256 devices in a mesh: ctx: 32 (over x, y, core), head: 8 (over z).
Axes of the slice: x: 4, y: 4, z: 8, core: 2. Of those that a mesh axis runs over, the one named last changes fastest.
Arguments:
- queries: bfloat16 [8192, 8192], P('ctx', 'head'), may hold values from -9 to 9
- cache_keys: bfloat16 [262144, 1024], P('ctx', 'head'), may hold values from -4.5 to 4.5
- cache_values: bfloat16 [262144, 1024], P('ctx', 'head'), may hold values from -4.5 to 4.5
- span_keys: bfloat16 [8192, 1024], P('ctx', 'head'), may hold values from -4.5 to 4.5
- span_values: bfloat16 [8192, 1024], P('ctx', 'head'), may hold values from -4.5 to 4.5
- selected: int32 [64, 24], replicated, may hold values from 0 to 2047, as said below
- counts: int32 [64], replicated, may hold values from 6 to 24, as said below
- out_weight: bfloat16 [8192, 8192], P('head', 'ctx'), may hold values from -0.0625 to 0.0625
Outputs:
- output: bfloat16 [8192, 8192], P('ctx', 'head')
The draws below stay inside these ranges and needn't reach their ends.
Inputs may be any that keep to these rules, and one draw needn't show every extreme that they name: `selected`: row b names the cache blocks of query block b. Its first counts[b] entries are distinct; the others are 0. Over the query blocks of one ctx index (blocks c * 2 to c * 2 + 1), at most 2 live entries name blocks of one ctx index's cache (blocks s * 64 to s * 64 + 63), and some pair reaches 2. `counts`: every query block of some ctx index has 24.
All inputs are finite; a program needn't handle non-finite values.
Results may differ from the reference program's by a relative error of at most 0.0057.
Values may be sent and summed in bfloat16 or wider, within the bound.
A program may use at most 128 MiB of HBM per device.

```python
import math
import jax
import jax.numpy as jnp
from jax import lax

D = 8192
HQ = 64
KVH = 8
HD = 128
BLK = 128
SEL = 24
CTX_DEV = 8192
TOKENS = 8192
CTX = 262144
QBLK = 64
NBLK = 2048
N_CTX = 32


def choose_blocks(key):
    qblocks = TOKENS // BLK
    blocks_dev = CTX_DEV // BLK
    qblocks_dev = qblocks // N_CTX
    count_key = jax.random.fold_in(key, 201)
    full_key = jax.random.fold_in(key, 202)
    perm_key = jax.random.fold_in(key, 203)
    start_key = jax.random.fold_in(key, 204)
    live_counts = jax.random.randint(count_key, (qblocks,), SEL // 4, SEL + 1)
    full_dest = jax.random.randint(full_key, (), 0, N_CTX)
    dest_index = jnp.arange(qblocks, dtype=jnp.int32) // qblocks_dev
    live_counts = jnp.where(dest_index == full_dest, SEL, live_counts).astype(jnp.int32)
    perm_keys = jax.random.split(perm_key, qblocks)
    owner_perms = jax.vmap(lambda one_key: jax.random.permutation(one_key, N_CTX))(perm_keys).astype(jnp.int32)
    shared_perm = jnp.take(owner_perms, full_dest * qblocks_dev, axis=0)
    owner_perms = jnp.where((dest_index == full_dest)[:, None], shared_perm[None, :], owner_perms)
    slot_index = jnp.arange(SEL, dtype=jnp.int32)
    owner_ids = owner_perms[:, slot_index % N_CTX]
    lap_index = slot_index // N_CTX
    start_table = jax.random.randint(start_key, (qblocks, N_CTX), 0, blocks_dev)
    start_ids = jnp.take_along_axis(start_table, owner_ids, axis=1)
    within = (start_ids + lap_index[None, :]) % blocks_dev
    block_ids = owner_ids * blocks_dev + within
    block_ids = jnp.where(slot_index[None, :] < live_counts[:, None], block_ids, 0)
    return (block_ids.astype(jnp.int32), live_counts)


def draw_selected(key, part):
    block_ids, live_counts = choose_blocks(key)
    return block_ids


def draw_counts(key, part):
    block_ids, live_counts = choose_blocks(key)
    return live_counts


def draw_queries(key, part):
    key = jax.random.fold_in(key, 1)
    base_draw = jnp.clip(jax.random.normal(key, (TOKENS, HQ * HD), jnp.float32), -4.5, 4.5)
    return base_draw.astype(jnp.bfloat16)


def draw_span_keys(key, part):
    key = jax.random.fold_in(key, 2)
    base_draw = jnp.clip(jax.random.normal(key, (TOKENS, KVH * HD), jnp.float32), -4.5, 4.5)
    return base_draw.astype(jnp.bfloat16)


def shard_levels(own_key, dims, cuts, low, top_value):
    def one(dim, parts):
        draws = jax.random.uniform(jax.random.fold_in(jax.random.fold_in(own_key, 6), dim), (parts,), jnp.float32, low / len(cuts), top_value / len(cuts))
        return jnp.repeat(jnp.exp(draws), dims[dim] // parts).reshape((-1,) + (1,) * (len(dims) - dim - 1))

    loudness = one(*cuts[0])
    for cut in cuts[1:]:
        loudness = loudness * one(*cut)
    return loudness


def scatter_about(key, extent, scale, reach, cuts=(), kind=jnp.bfloat16):
    values = scale * jax.random.normal(key, extent, jnp.float32)
    if cuts:
        values = values * shard_levels(key, extent, cuts, -0.22, 0.18)
    return jnp.clip(values, -reach, reach).astype(kind)


def setup_inputs(seed: int = 0) -> dict:
    streams_of = jax.random.split(jax.random.key(seed), 9)
    return {
        "queries": draw_queries(jax.random.fold_in(streams_of[8], 71), 0),
        "cache_keys": scatter_about(streams_of[1], (CTX, KVH * HD), 1.0, 4.5, ((0, 32), (1, 8))),
        "cache_values": scatter_about(streams_of[2], (CTX, KVH * HD), 1.0, 4.5, ((0, 32), (1, 8))),
        "span_keys": draw_span_keys(jax.random.fold_in(streams_of[8], 71), 0),
        "span_values": scatter_about(streams_of[4], (TOKENS, KVH * HD), 1.0, 4.5, ((0, 32), (1, 8))),
        "selected": draw_selected(jax.random.fold_in(streams_of[8], 71), 0),
        "counts": draw_counts(jax.random.fold_in(streams_of[8], 71), 0),
        "out_weight": scatter_about(streams_of[7], (HQ * HD, D), (HQ * HD) ** -0.5, 0.0625, ((0, 8), (1, 32))),
    }


def reference(queries, cache_keys, cache_values, span_keys, span_values, selected, counts, out_weight):
    q_group = HQ // KVH
    key_blocks = cache_keys.reshape(NBLK, BLK, KVH, HD)
    value_blocks = cache_values.reshape(NBLK, BLK, KVH, HD)
    score_scale = 1.0 / math.sqrt(HD)
    key_total = SEL * BLK + BLK
    key_index = jnp.arange(key_total, dtype=jnp.int32)
    row_index = jnp.arange(BLK, dtype=jnp.int32)

    def one_block(block_items):
        q_block, own_keys, own_values, sel_row, live_count = block_items
        sel_keys = jnp.take(key_blocks, sel_row, axis=0).reshape(SEL * BLK, KVH, HD)
        sel_values = jnp.take(value_blocks, sel_row, axis=0).reshape(SEL * BLK, KVH, HD)
        keys_all = jnp.concatenate([sel_keys, own_keys.reshape(BLK, KVH, HD)], axis=0).astype(jnp.float32)
        values_all = jnp.concatenate([sel_values, own_values.reshape(BLK, KVH, HD)], axis=0).astype(jnp.float32)
        q_float = q_block.reshape(BLK, KVH, q_group, HD).astype(jnp.float32)
        scores = jnp.einsum('tgrd,kgd->gtrk', q_float, keys_all) * score_scale
        sel_part = (key_index < SEL * BLK) & (key_index // BLK < live_count)
        own_part = (key_index >= SEL * BLK) & ((key_index - SEL * BLK)[None, :] <= row_index[:, None])
        allowed = sel_part[None, :] | own_part
        scores = jnp.where(allowed[None, :, None, :], scores, -jnp.inf)
        row_max = lax.optimization_barrier(jnp.max(scores, axis=-1))
        weights = jnp.exp(scores - row_max[..., None])
        row_sum = lax.optimization_barrier(jnp.sum(weights, axis=-1))
        weights_bf = weights.astype(jnp.bfloat16)
        weighted = jnp.einsum('gtrk,kgd->gtrd', weights_bf.astype(jnp.float32), values_all)
        result = weighted / row_sum[..., None]
        return jnp.transpose(result, (1, 0, 2, 3)).reshape(BLK, HQ * HD).astype(jnp.bfloat16)
    attention = lax.map(one_block, (queries.reshape(QBLK, BLK, HQ * HD), span_keys.reshape(QBLK, BLK, KVH * HD), span_values.reshape(QBLK, BLK, KVH * HD), selected, counts)).reshape(TOKENS, HQ * HD)
    return jnp.dot(attention, out_weight, preferred_element_type=jnp.float32).astype(jnp.bfloat16)
```

```python
import functools
import math

import jax
import jax.numpy as jnp
from jax import lax
from jax.experimental import pallas as pl
from jax.experimental.pallas import tpu as pltpu
from jax.sharding import PartitionSpec as P

HD = 128
BLK = 128
SEL = 24
GROUP = 8
NX = 4
NY = 4
NZ = 8
NCTX = 32
CBLK = 64
PAIRS = SEL // 2
MESH = pl.DeviceIdType.MESH
EXP_SCALE = math.log2(math.e) / math.sqrt(HD)

NEAR = [(1, 0), (3, 0), (0, 1), (0, 3)]
DIAG = [(1, 1), (3, 3), (1, 3), (3, 1)]
FAR = [(2, 0), (0, 2), (2, 1), (1, 2), (2, 3), (3, 2), (2, 2)]
KV_ORDER = [(a, b, k) for g in (NEAR, DIAG, FAR) for k in (0, 1) for a, b in g] + [(0, 0, 1)]


def weight_plan():
    plan = {}
    for path in ("a", "b"):
        base = 0 if path == "a" else 512

        def at(u, v, path=path):
            return (u, v) if path == "a" else (v, u)

        for s in (1, -1):
            plan[path, 1, 0, s] = (at(0, 0), base, 512, at(s, 0))
            quarter = base if s == 1 else base + 256
            plan[path, 2, 0, s] = (at(-s, 0), quarter, 256, at(s, 0))
            for u in (0, -1, 1, 2):
                plan[path, 3, u, s] = (at(u, 0), base, 512, at(0, s))
                plan[path, 4, u, s] = (at(u, -s), quarter, 256, at(0, s))
    return plan


PLAN = weight_plan()
PLAN_ID = {name: n for n, name in enumerate(PLAN)}
SIB = {}
for _path in ("a", "b"):
    for _u in range(-1, 3):
        for _v in range(-1, 3):
            if (_u, _v) != (0, 0):
                SIB[_path, _u, _v] = len(SIB) + 1


def body(
    meta, q_hbm, ck_hbm, cv_hbm, sk_hbm, sv_hbm, w_hbm, o_ref,
    kc, vc, qv, skv, svv, outgo, income, wfull, attn, q8, scores, own_scores, mx, lsum, acc,
    load_sem, kv_send, kv_recv, perm_sem, w_send, w_recv, s_send, s_recv, a_send, a_recv,
):
    c = lax.axis_index("ctx")
    z = lax.axis_index("head")
    x = c // 8
    y = (c // 2) % 4
    k = c % 2

    loads = [
        pltpu.make_async_copy(src, dst, load_sem.at[n])
        for n, (src, dst) in enumerate(
            ((ck_hbm, kc), (cv_hbm, vc), (q_hbm, qv), (sk_hbm, skv), (sv_hbm, svv))
        )
    ]
    for cp in loads:
        cp.start()

    def ctx_at(dx, dy, dk=0):
        return ((x + dx + NX) % NX) * 8 + ((y + dy + NY) % NY) * 2 + (k + dk) % 2

    pz = c // 4
    pb = (c // 2) % 2
    perm_to = (4 * ((pz + z) % NZ) + 2 * pb + k, pz)
    perm_from = (4 * z + 2 * pb + k, (pz - z + NZ) % NZ)
    perm_self = (pz == z) & (z == 0)

    barrier = pltpu.get_barrier_semaphore()

    def greet(i, carry):
        pl.semaphore_signal(barrier, inc=1, device_id=((c + i) % NCTX, z), device_id_type=MESH)
        return carry

    lax.fori_loop(1, NCTX, greet, 0)
    for dz in (1, NZ - 1):
        pl.semaphore_signal(barrier, inc=1, device_id=(c, (z + dz) % NZ), device_id_type=MESH)

    @pl.when(jnp.logical_not(perm_self))
    def _():
        pl.semaphore_signal(barrier, inc=1, device_id=perm_to, device_id_type=MESH)
        pl.semaphore_signal(barrier, inc=1, device_id=perm_from, device_id_type=MESH)

    pl.semaphore_wait(barrier, jnp.where(perm_self, NCTX + 1, NCTX + 3))

    def slot(dx, dy, lane=None):
        xy = ((x + dx + NX) % NX) * NY + (y + dy + NY) % NY
        return (xy // 2 - z + NZ) % NZ, 2 * (xy % 2) + (k if lane is None else lane)

    perm_remote = pltpu.make_async_remote_copy(
        src_ref=w_hbm, dst_ref=wfull.at[z, 2 * pb + k], send_sem=perm_sem.at[0],
        recv_sem=perm_sem.at[1], device_id=perm_to, device_id_type=MESH,
    )
    perm_local = pltpu.make_async_copy(w_hbm, wfull.at[z, 2 * pb + k], perm_sem.at[1])

    @pl.when(perm_self)
    def _():
        perm_local.start()

    @pl.when(jnp.logical_not(perm_self))
    def _():
        perm_remote.start()

    loads[0].wait()
    loads[1].wait()

    def kv_copy(d, source):
        return pltpu.make_async_remote_copy(
            src_ref=outgo.at[d], dst_ref=income.at[source], send_sem=kv_send.at[d],
            recv_sem=kv_recv.at[source], device_id=(d, z), device_id_type=MESH,
        )

    for dx, dy, dk in KV_ORDER:
        d = ctx_at(dx, dy, dk)
        for r in range(2):
            blk = meta[2 * d + r]
            outgo[d, r, 0] = kc[blk]
            outgo[d, r, 1] = vc[blk]
        kv_copy(d, c).start()
    for r in range(2):
        blk = meta[2 * c + r]
        income[c, r, 0] = kc[blk]
        income[c, r, 1] = vc[blk]
    loads[2].wait()
    loads[3].wait()
    loads[4].wait()

    def w_copy(name):
        (dx, dy), row, rows, (tx, ty) = PLAN[name]
        zp, bk = slot(dx, dy)
        piece = wfull.at[zp, bk, pl.ds(row, rows)]
        n = PLAN_ID[name]
        return pltpu.make_async_remote_copy(
            src_ref=piece, dst_ref=piece, send_sem=w_send.at[n], recv_sem=w_recv.at[n],
            device_id=(ctx_at(tx, ty), z), device_id_type=MESH,
        )

    def w_arrived(name):
        (dx, dy), row, rows, (tx, ty) = PLAN[name]
        zp, bk = slot(dx - tx, dy - ty)
        piece = wfull.at[zp, bk, pl.ds(row, rows)]
        n = PLAN_ID[name]
        pltpu.make_async_remote_copy(
            src_ref=piece, dst_ref=piece, send_sem=w_send.at[n], recv_sem=w_recv.at[n],
            device_id=(ctx_at(tx, ty), z), device_id_type=MESH,
        ).wait_recv()

    def s_copy(name, lane):
        if name is None:
            n, (u, v), row, rows = 0, (0, 0), 0, 1024
        else:
            n, (u, v), row, rows = SIB[name], name[1:], (0 if name[0] == "a" else 512), 512
        zp, bk = slot(u, v, lane)
        piece = wfull.at[zp, bk, pl.ds(row, rows)]
        return pltpu.make_async_remote_copy(
            src_ref=piece, dst_ref=piece, send_sem=s_send.at[n], recv_sem=s_recv.at[n],
            device_id=(ctx_at(0, 0, 1), z), device_id_type=MESH,
        )

    def s_start(path, u, v):
        name = (path, u, v) if path == "a" else (path, v, u)
        s_copy(name, k).start()

    def a_ref(s, hop, b, sending):
        off = -s * hop if sending else -s * (hop + 1)
        src = attn.at[(z + off + 2 * NZ) % NZ, b]
        if hop == 3:
            src = src.at[pl.ds(0 if s == 1 else 64, 64)]
        return src

    def a_copy(s, hop, b, sending=True):
        n = (b * 4 + hop) * 2 + (0 if s == 1 else 1)
        ref = a_ref(s, hop, b, sending)
        return pltpu.make_async_remote_copy(
            src_ref=ref, dst_ref=ref, send_sem=a_send.at[n], recv_sem=a_recv.at[n],
            device_id=(c, (z + s + NZ) % NZ), device_id_type=MESH,
        )

    def a_start(hop, b):
        for s in (1, -1):
            if hop:
                a_copy(s, hop - 1, b, False).wait_recv()
            a_copy(s, hop, b).start()

    def kv_sent(i, carry):
        d = (c + i) % NCTX
        kv_copy(d, c).wait_send()
        return carry

    lax.fori_loop(1, NCTX, kv_sent, 0)

    own_zp, own_bk = slot(0, 0)

    pltpu.make_async_copy(w_hbm, wfull.at[own_zp, own_bk], perm_sem.at[1]).wait()
    for s in (1, -1):
        for path in ("a", "b"):
            w_copy((path, 1, 0, s)).start()
    for s in (1, -1):
        for path in ("a", "b"):
            w_copy((path, 3, 0, s)).start()
    s_copy(None, k).start()

    def kv_landed(i, carry):
        src = (c + i) % NCTX
        kv_copy(c, src).wait_recv()
        return carry

    lax.fori_loop(1, NCTX, kv_landed, 0)

    causal = lax.broadcasted_iota(jnp.int32, (BLK, BLK), 1) <= lax.broadcasted_iota(
        jnp.int32, (BLK, BLK), 0
    )
    nt = (((1,), (1,)), ((), ()))

    def attend(b):
        for h in range(GROUP):
            q8[pl.ds(h * BLK, BLK), :] = qv[pl.ds(b * BLK, BLK), pl.ds(h * HD, HD)]
        own_k = skv[pl.ds(b * BLK, BLK), :]
        own_v = svv[pl.ds(b * BLK, BLK), :]
        for h in range(GROUP):
            rows = pl.ds(h * BLK, BLK)
            s_own = lax.dot_general(q8[rows, :], own_k, nt, preferred_element_type=jnp.float32)
            s_own = jnp.where(causal, s_own, -jnp.inf)
            own_scores[rows, :] = s_own
            mx[rows, :] = s_own

        def score_pair(p, carry):
            i0 = meta[2 * NCTX + b * SEL + 2 * p]
            i1 = meta[2 * NCTX + b * SEL + 2 * p + 1]
            keys = jnp.concatenate([income[i0 // 2, i0 % 2, 0], income[i1 // 2, i1 % 2, 0]], axis=0)
            for h in range(GROUP):
                rows = pl.ds(h * BLK, BLK)
                s = lax.dot_general(q8[rows, :], keys, nt, preferred_element_type=jnp.float32)
                scores[p, rows, :] = s
                mx[rows, :] = jnp.maximum(mx[rows, :], jnp.maximum(s[:, :BLK], s[:, BLK:]))
            return carry

        lax.fori_loop(0, PAIRS, score_pair, 0)

        for h in range(GROUP):
            rows = pl.ds(h * BLK, BLK)
            top = jnp.max(mx[rows, :], axis=1, keepdims=True) * EXP_SCALE
            top = jnp.broadcast_to(top, (BLK, BLK))
            mx[rows, :] = top
            w = jnp.exp2(own_scores[rows, :] * EXP_SCALE - top)
            lsum[rows, :] = w
            acc[rows, :] = jnp.dot(
                w.astype(jnp.bfloat16), own_v, preferred_element_type=jnp.float32
            )

        live = meta[2 * NCTX + 2 * SEL + b]

        def value_pair(p, carry):
            i0 = meta[2 * NCTX + b * SEL + 2 * p]
            i1 = meta[2 * NCTX + b * SEL + 2 * p + 1]
            vals = jnp.concatenate([income[i0 // 2, i0 % 2, 1], income[i1 // 2, i1 % 2, 1]], axis=0)
            off0 = jnp.where(2 * p < live, 0.0, 1e30).astype(jnp.float32)
            off1 = jnp.where(2 * p + 1 < live, 0.0, 1e30).astype(jnp.float32)
            for h in range(GROUP):
                rows = pl.ds(h * BLK, BLK)
                top = mx[rows, :]
                s = scores[p, rows, :]
                w0 = jnp.exp2(s[:, :BLK] * EXP_SCALE - (top + off0))
                w1 = jnp.exp2(s[:, BLK:] * EXP_SCALE - (top + off1))
                lsum[rows, :] = lsum[rows, :] + (w0 + w1)
                w = jnp.concatenate([w0.astype(jnp.bfloat16), w1.astype(jnp.bfloat16)], axis=1)
                acc[rows, :] = acc[rows, :] + jnp.dot(w, vals, preferred_element_type=jnp.float32)
            return carry

        lax.fori_loop(0, PAIRS, value_pair, 0)
        for h in range(GROUP):
            rows = pl.ds(h * BLK, BLK)
            total = jnp.sum(lsum[rows, :], axis=1, keepdims=True)
            attn[z, b, :, pl.ds(h * HD, HD)] = (acc[rows, :] / total).astype(jnp.bfloat16)

    attend(0)
    a_start(0, 0)

    for path in ("a", "b"):
        for s in (1, -1):
            w_arrived((path, 1, 0, s))
            w_copy((path, 2, 0, s)).start()
    for path in ("a", "b"):
        for u in (-1, 1):
            for s in (1, -1):
                w_copy((path, 3, u, s)).start()
            s_start(path, u, 0)

    attend(1)
    a_start(0, 1)
    a_start(1, 0)

    def w_far():
        for path in ("a", "b"):
            for s in (1, -1):
                w_arrived((path, 2, 0, s))
        for path in ("a", "b"):
            for s in (1, -1):
                w_copy((path, 3, 2, s)).start()
            s_start(path, 2, 0)

    def w_pass(u):
        for path in ("a", "b"):
            for s in (1, -1):
                w_arrived((path, 3, u, s))
                w_copy((path, 4, u, s)).start()
                s_start(path, u, -s)

    w_pass(0)
    w_far()
    a_start(1, 1)
    a_start(2, 0)
    w_pass(-1)
    a_start(2, 1)
    w_pass(1)
    a_start(3, 0)
    w_pass(2)
    a_start(3, 1)
    for u in (0, -1, 1, 2):
        for path in ("a", "b"):
            for s in (1, -1):
                w_arrived((path, 4, u, s))
            s_start(path, u, 2)

    s_copy(None, 1 - k).wait_recv()
    for name in SIB:
        s_copy(name, 1 - k).wait_recv()
    for b in range(2):
        for s in (1, -1):
            a_copy(s, 3, b, False).wait_recv()

    for bk in range(4):
        def add(zp, total, bk=bk):
            return total + jnp.dot(
                attn[zp].reshape(2 * BLK, GROUP * HD), wfull[zp, bk],
                preferred_element_type=jnp.float32,
            )

        total = lax.fori_loop(0, NZ, add, jnp.zeros((2 * BLK, 256), jnp.float32))
        o_ref[:, pl.ds(bk * 256, 256)] = total.astype(jnp.bfloat16)

    @pl.when(jnp.logical_not(perm_self))
    def _():
        perm_remote.wait_send()

    for name in PLAN:
        w_copy(name).wait_send()
    s_copy(None, k).wait_send()
    for name in SIB:
        s_copy(name, k).wait_send()
    for b in range(2):
        for hop in range(4):
            for s in (1, -1):
                a_copy(s, hop, b).wait_send()


def per_device(
    queries, cache_keys, cache_values, span_keys, span_values, selected, counts, out_weight
):
    c = lax.axis_index("ctx")
    sel = selected.reshape(NCTX, 2, SEL)
    cnt = counts.reshape(NCTX, 2, 1)
    live = lax.broadcasted_iota(jnp.int32, sel.shape, 2) < cnt
    entry = lax.broadcasted_iota(jnp.int32, sel.shape, 1) * SEL + lax.broadcasted_iota(
        jnp.int32, sel.shape, 2
    )
    key = jnp.where(live & ((sel >> 6) == c), entry * CBLK + (sel & (CBLK - 1)), -1)
    first = jnp.min(jnp.where(key < 0, 2 * SEL * CBLK, key), axis=(1, 2))
    last = jnp.max(jnp.maximum(key, 0), axis=(1, 2))
    send = (jnp.stack((first, last), axis=1) & (CBLK - 1)).reshape(2 * NCTX)

    mine = lax.dynamic_slice_in_dim(selected, 2 * c, 2, 0)
    my_cnt = lax.dynamic_slice_in_dim(counts, 2 * c, 2, 0)
    my_live = (lax.broadcasted_iota(jnp.int32, (2, SEL), 1) < my_cnt[:, None]).reshape(2 * SEL)
    owner = (mine >> 6).reshape(2 * SEL)
    order = jnp.arange(2 * SEL, dtype=jnp.int32)
    earlier = (
        (owner[:, None] == owner[None, :]) & my_live[None, :] & (order[None, :] < order[:, None])
    )
    place = owner * 2 + jnp.any(earlier, axis=1).astype(jnp.int32)
    lead = jnp.broadcast_to(place.reshape(2, SEL)[:, :1], (2, SEL)).reshape(2 * SEL)
    place = jnp.where(my_live, place, lead)
    meta = jnp.concatenate((send, place, my_cnt))

    vmem = pltpu.VMEM
    bf16 = jnp.bfloat16
    f32 = jnp.float32
    dma = pltpu.SemaphoreType.DMA
    hbm = pl.BlockSpec(memory_space=pl.ANY)
    return pl.pallas_call(
        body,
        out_shape=jax.ShapeDtypeStruct((2 * BLK, GROUP * HD), bf16),
        in_specs=[pl.BlockSpec(memory_space=pltpu.SMEM)] + [hbm] * 6,
        out_specs=pl.BlockSpec(memory_space=vmem),
        scratch_shapes=[
            vmem((CBLK, BLK, HD), bf16),
            vmem((CBLK, BLK, HD), bf16),
            vmem((2 * BLK, GROUP * HD), bf16),
            vmem((2 * BLK, HD), bf16),
            vmem((2 * BLK, HD), bf16),
            vmem((NCTX, 2, 2, BLK, HD), bf16),
            vmem((NCTX, 2, 2, BLK, HD), bf16),
            vmem((NZ, 4, 1024, 256), bf16),
            vmem((NZ, 2, BLK, GROUP * HD), bf16),
            vmem((GROUP * BLK, HD), bf16),
            vmem((PAIRS, GROUP * BLK, 2 * BLK), f32),
            vmem((GROUP * BLK, BLK), f32),
            vmem((GROUP * BLK, BLK), f32),
            vmem((GROUP * BLK, BLK), f32),
            vmem((GROUP * BLK, HD), f32),
            dma((5,)),
            dma((NCTX,)),
            dma((NCTX,)),
            dma((2,)),
            dma((len(PLAN),)),
            dma((len(PLAN),)),
            dma((len(SIB) + 1,)),
            dma((len(SIB) + 1,)),
            dma((16,)),
            dma((16,)),
        ],
        compiler_params=pltpu.CompilerParams(
            collective_id=0, has_side_effects=True, vmem_limit_bytes=58 * 2**20
        ),
        cost_estimate=pl.CostEstimate(
            flops=8_000_000_000, bytes_accessed=30_000_000, transcendentals=7_000_000
        ),
        name="sparse_attention_projection",
    )(
        meta,
        queries,
        cache_keys.reshape(CBLK, BLK, HD),
        cache_values.reshape(CBLK, BLK, HD),
        span_keys,
        span_values,
        out_weight,
    )


def solution(mesh):
    placed = (
        P("ctx", "head"),
        P("ctx", "head"),
        P("ctx", "head"),
        P("ctx", "head"),
        P("ctx", "head"),
        P(),
        P(),
        P("head", "ctx"),
    )
    return jax.shard_map(
        per_device, mesh=mesh, in_specs=placed, out_specs=P("ctx", "head"), check_vma=False
    )
```

```python
import functools
import math

import jax
import jax.numpy as jnp
from jax import lax
from jax.experimental import pallas as pl
from jax.experimental.pallas import tpu as pltpu
from jax.sharding import PartitionSpec as P

HD = 128
BLK = 128
SEL = 24
GROUP = 8
NX = 4
NY = 4
NZ = 8
NCTX = 32
CBLK = 64
PAIRS = SEL // 2
MESH = pl.DeviceIdType.MESH
EXP_SCALE = math.log2(math.e) / math.sqrt(HD)

NEAR = [(1, 0), (3, 0), (0, 1), (0, 3)]
DIAG = [(1, 1), (3, 3), (1, 3), (3, 1)]
FAR = [(2, 0), (0, 2), (2, 1), (1, 2), (2, 3), (3, 2), (2, 2)]
KV_ORDER = [(a, b, k) for g in (NEAR, DIAG, FAR) for k in (0, 1) for a, b in g] + [(0, 0, 1)]


def weight_plan():
    plan = {}
    for path in ("a", "b"):
        base = 0 if path == "a" else 512

        def at(u, v, path=path):
            return (u, v) if path == "a" else (v, u)

        for s in (1, -1):
            plan[path, 1, 0, s] = (at(0, 0), base, 512, at(s, 0))
            quarter = base if s == 1 else base + 256
            plan[path, 2, 0, s] = (at(-s, 0), quarter, 256, at(s, 0))
            for u in (0, -1, 1, 2):
                plan[path, 3, u, s] = (at(u, 0), base, 512, at(0, s))
                plan[path, 4, u, s] = (at(u, -s), quarter, 256, at(0, s))
    return plan


PLAN = weight_plan()
PLAN_ID = {name: n for n, name in enumerate(PLAN)}
SIB = {}
for _path in ("a", "b"):
    for _u in range(-1, 3):
        for _v in range(-1, 3):
            if (_u, _v) != (0, 0):
                SIB[_path, _u, _v] = len(SIB) + 1


def body(
    meta, q_hbm, ck_hbm, cv_hbm, sk_hbm, sv_hbm, w_hbm, o_ref,
    kc, vc, qv, skv, svv, outgo, income, wtmp, wfull, attn, q8, scores, own_scores, mx, lsum, acc,
    load_sem, kv_send, kv_recv, perm_sem, w_send, w_recv, s_send, s_recv, a_send, a_recv,
):
    c = lax.axis_index("ctx")
    z = lax.axis_index("head")
    x = c // 8
    y = (c // 2) % 4
    k = c % 2

    loads = [
        pltpu.make_async_copy(src, dst, load_sem.at[n])
        for n, (src, dst) in enumerate(
            ((ck_hbm, kc), (cv_hbm, vc), (q_hbm, qv), (sk_hbm, skv), (sv_hbm, svv))
        )
    ]
    for cp in loads:
        cp.start()

    def ctx_at(dx, dy, dk=0):
        return ((x + dx + NX) % NX) * 8 + ((y + dy + NY) % NY) * 2 + (k + dk) % 2

    pb = (c // 2) % 2
    in_plane = 4 * ((c // 4 + z) % NZ) + 2 * pb + k
    in_self = z == 0
    to_z = (c // 4 - z + NZ) % NZ
    z_self = to_z == z

    barrier = pltpu.get_barrier_semaphore()

    def greet(i, carry):
        pl.semaphore_signal(barrier, inc=1, device_id=((c + i) % NCTX, z), device_id_type=MESH)
        return carry

    lax.fori_loop(1, NCTX, greet, 0)
    for dz in (1, NZ - 1):
        pl.semaphore_signal(barrier, inc=1, device_id=(c, (z + dz) % NZ), device_id_type=MESH)

    @pl.when(jnp.logical_not(z_self))
    def _():
        pl.semaphore_signal(barrier, inc=1, device_id=(c, to_z), device_id_type=MESH)

    pl.semaphore_wait(barrier, jnp.where(z_self, NCTX + 1, NCTX + 2))

    def slot(dx, dy, lane=None):
        xy = ((x + dx + NX) % NX) * NY + (y + dy + NY) % NY
        return (xy // 2 - z + NZ) % NZ, 2 * (xy % 2) + (k if lane is None else lane)

    move_in = pltpu.make_async_remote_copy(
        src_ref=w_hbm, dst_ref=wtmp, send_sem=perm_sem.at[0], recv_sem=perm_sem.at[1],
        device_id=(in_plane, z), device_id_type=MESH,
    )
    keep_in = pltpu.make_async_copy(w_hbm, wtmp, perm_sem.at[1])
    own_piece = wfull.at[z, 2 * pb + k]
    move_z = pltpu.make_async_remote_copy(
        src_ref=wtmp, dst_ref=own_piece, send_sem=perm_sem.at[2], recv_sem=perm_sem.at[3],
        device_id=(c, to_z), device_id_type=MESH,
    )
    keep_z = pltpu.make_async_copy(wtmp, own_piece, perm_sem.at[3])

    def either(flag, one, other):
        pl.when(flag)(one)
        pl.when(jnp.logical_not(flag))(other)

    either(in_self, keep_in.start, move_in.start)

    loads[0].wait()
    loads[1].wait()

    def kv_copy(d, source):
        return pltpu.make_async_remote_copy(
            src_ref=outgo.at[d], dst_ref=income.at[source], send_sem=kv_send.at[d],
            recv_sem=kv_recv.at[source], device_id=(d, z), device_id_type=MESH,
        )

    for dx, dy, dk in KV_ORDER:
        d = ctx_at(dx, dy, dk)
        for r in range(2):
            blk = meta[2 * d + r]
            outgo[d, r, 0] = kc[blk]
            outgo[d, r, 1] = vc[blk]
        kv_copy(d, c).start()
    for r in range(2):
        blk = meta[2 * c + r]
        income[c, r, 0] = kc[blk]
        income[c, r, 1] = vc[blk]
    keep_in.wait()
    either(z_self, keep_z.start, move_z.start)
    loads[2].wait()
    loads[3].wait()
    loads[4].wait()

    def w_copy(name):
        (dx, dy), row, rows, (tx, ty) = PLAN[name]
        zp, bk = slot(dx, dy)
        piece = wfull.at[zp, bk, pl.ds(row, rows)]
        n = PLAN_ID[name]
        return pltpu.make_async_remote_copy(
            src_ref=piece, dst_ref=piece, send_sem=w_send.at[n], recv_sem=w_recv.at[n],
            device_id=(ctx_at(tx, ty), z), device_id_type=MESH,
        )

    def w_arrived(name):
        (dx, dy), row, rows, (tx, ty) = PLAN[name]
        zp, bk = slot(dx - tx, dy - ty)
        piece = wfull.at[zp, bk, pl.ds(row, rows)]
        n = PLAN_ID[name]
        pltpu.make_async_remote_copy(
            src_ref=piece, dst_ref=piece, send_sem=w_send.at[n], recv_sem=w_recv.at[n],
            device_id=(ctx_at(tx, ty), z), device_id_type=MESH,
        ).wait_recv()

    def s_copy(name, lane):
        if name is None:
            n, (u, v), row, rows = 0, (0, 0), 0, 1024
        else:
            n, (u, v), row, rows = SIB[name], name[1:], (0 if name[0] == "a" else 512), 512
        zp, bk = slot(u, v, lane)
        piece = wfull.at[zp, bk, pl.ds(row, rows)]
        return pltpu.make_async_remote_copy(
            src_ref=piece, dst_ref=piece, send_sem=s_send.at[n], recv_sem=s_recv.at[n],
            device_id=(ctx_at(0, 0, 1), z), device_id_type=MESH,
        )

    def s_start(path, u, v):
        name = (path, u, v) if path == "a" else (path, v, u)
        s_copy(name, k).start()

    def a_ref(s, hop, b, sending):
        off = -s * hop if sending else -s * (hop + 1)
        src = attn.at[(z + off + 2 * NZ) % NZ, b]
        if hop == 3:
            src = src.at[pl.ds(0 if s == 1 else 64, 64)]
        return src

    def a_copy(s, hop, b, sending=True):
        n = (b * 4 + hop) * 2 + (0 if s == 1 else 1)
        ref = a_ref(s, hop, b, sending)
        return pltpu.make_async_remote_copy(
            src_ref=ref, dst_ref=ref, send_sem=a_send.at[n], recv_sem=a_recv.at[n],
            device_id=(c, (z + s + NZ) % NZ), device_id_type=MESH,
        )

    def a_start(hop, b):
        for s in (1, -1):
            if hop:
                a_copy(s, hop - 1, b, False).wait_recv()
            a_copy(s, hop, b).start()

    def kv_sent(i, carry):
        d = (c + i) % NCTX
        kv_copy(d, c).wait_send()
        return carry

    lax.fori_loop(1, NCTX, kv_sent, 0)

    own_zp, own_bk = slot(0, 0)

    pltpu.make_async_copy(wtmp, wfull.at[own_zp, own_bk], perm_sem.at[3]).wait()
    for s in (1, -1):
        for path in ("a", "b"):
            w_copy((path, 1, 0, s)).start()
    for s in (1, -1):
        for path in ("a", "b"):
            w_copy((path, 3, 0, s)).start()
    s_copy(None, k).start()

    def kv_landed(i, carry):
        src = (c + i) % NCTX
        kv_copy(c, src).wait_recv()
        return carry

    lax.fori_loop(1, NCTX, kv_landed, 0)

    causal = lax.broadcasted_iota(jnp.int32, (BLK, BLK), 1) <= lax.broadcasted_iota(
        jnp.int32, (BLK, BLK), 0
    )
    nt = (((1,), (1,)), ((), ()))

    def attend(b):
        for h in range(GROUP):
            q8[pl.ds(h * BLK, BLK), :] = qv[pl.ds(b * BLK, BLK), pl.ds(h * HD, HD)]
        own_k = skv[pl.ds(b * BLK, BLK), :]
        own_v = svv[pl.ds(b * BLK, BLK), :]
        for h in range(GROUP):
            rows = pl.ds(h * BLK, BLK)
            s_own = lax.dot_general(q8[rows, :], own_k, nt, preferred_element_type=jnp.float32)
            s_own = jnp.where(causal, s_own, -jnp.inf)
            own_scores[rows, :] = s_own
            mx[rows, :] = s_own

        def score_pair(p, carry):
            i0 = meta[2 * NCTX + b * SEL + 2 * p]
            i1 = meta[2 * NCTX + b * SEL + 2 * p + 1]
            keys = jnp.concatenate([income[i0 // 2, i0 % 2, 0], income[i1 // 2, i1 % 2, 0]], axis=0)
            for h in range(GROUP):
                rows = pl.ds(h * BLK, BLK)
                s = lax.dot_general(q8[rows, :], keys, nt, preferred_element_type=jnp.float32)
                scores[p, rows, :] = s
                mx[rows, :] = jnp.maximum(mx[rows, :], jnp.maximum(s[:, :BLK], s[:, BLK:]))
            return carry

        lax.fori_loop(0, PAIRS, score_pair, 0)

        for h in range(GROUP):
            rows = pl.ds(h * BLK, BLK)
            top = jnp.max(mx[rows, :], axis=1, keepdims=True) * EXP_SCALE
            top = jnp.broadcast_to(top, (BLK, BLK))
            mx[rows, :] = top
            w = jnp.exp2(own_scores[rows, :] * EXP_SCALE - top)
            lsum[rows, :] = w
            acc[rows, :] = jnp.dot(
                w.astype(jnp.bfloat16), own_v, preferred_element_type=jnp.float32
            )

        live = meta[2 * NCTX + 2 * SEL + b]

        def value_pair(p, carry):
            i0 = meta[2 * NCTX + b * SEL + 2 * p]
            i1 = meta[2 * NCTX + b * SEL + 2 * p + 1]
            vals = jnp.concatenate([income[i0 // 2, i0 % 2, 1], income[i1 // 2, i1 % 2, 1]], axis=0)
            off0 = jnp.where(2 * p < live, 0.0, 1e30).astype(jnp.float32)
            off1 = jnp.where(2 * p + 1 < live, 0.0, 1e30).astype(jnp.float32)
            for h in range(GROUP):
                rows = pl.ds(h * BLK, BLK)
                top = mx[rows, :]
                s = scores[p, rows, :]
                w0 = jnp.exp2(s[:, :BLK] * EXP_SCALE - (top + off0))
                w1 = jnp.exp2(s[:, BLK:] * EXP_SCALE - (top + off1))
                lsum[rows, :] = lsum[rows, :] + (w0 + w1)
                w = jnp.concatenate([w0.astype(jnp.bfloat16), w1.astype(jnp.bfloat16)], axis=1)
                acc[rows, :] = acc[rows, :] + jnp.dot(w, vals, preferred_element_type=jnp.float32)
            return carry

        lax.fori_loop(0, PAIRS, value_pair, 0)
        for h in range(GROUP):
            rows = pl.ds(h * BLK, BLK)
            total = jnp.sum(lsum[rows, :], axis=1, keepdims=True)
            attn[z, b, :, pl.ds(h * HD, HD)] = (acc[rows, :] / total).astype(jnp.bfloat16)

    attend(0)
    a_start(0, 0)

    for path in ("a", "b"):
        for s in (1, -1):
            w_arrived((path, 1, 0, s))
            w_copy((path, 2, 0, s)).start()
    for path in ("a", "b"):
        for u in (-1, 1):
            for s in (1, -1):
                w_copy((path, 3, u, s)).start()
            s_start(path, u, 0)

    attend(1)
    a_start(0, 1)
    a_start(1, 0)

    def w_far():
        for path in ("a", "b"):
            for s in (1, -1):
                w_arrived((path, 2, 0, s))
        for path in ("a", "b"):
            for s in (1, -1):
                w_copy((path, 3, 2, s)).start()
            s_start(path, 2, 0)

    def w_pass(u):
        for path in ("a", "b"):
            for s in (1, -1):
                w_arrived((path, 3, u, s))
                w_copy((path, 4, u, s)).start()
                s_start(path, u, -s)

    w_pass(0)
    w_far()
    a_start(1, 1)
    a_start(2, 0)
    w_pass(-1)
    a_start(2, 1)
    w_pass(1)
    a_start(3, 0)
    w_pass(2)
    a_start(3, 1)
    for u in (0, -1, 1, 2):
        for path in ("a", "b"):
            for s in (1, -1):
                w_arrived((path, 4, u, s))
            s_start(path, u, 2)

    s_copy(None, 1 - k).wait_recv()
    for name in SIB:
        s_copy(name, 1 - k).wait_recv()
    for b in range(2):
        for s in (1, -1):
            a_copy(s, 3, b, False).wait_recv()

    for bk in range(4):
        def add(zp, total, bk=bk):
            return total + jnp.dot(
                attn[zp].reshape(2 * BLK, GROUP * HD), wfull[zp, bk],
                preferred_element_type=jnp.float32,
            )

        total = lax.fori_loop(0, NZ, add, jnp.zeros((2 * BLK, 256), jnp.float32))
        o_ref[:, pl.ds(bk * 256, 256)] = total.astype(jnp.bfloat16)

    pl.when(jnp.logical_not(in_self))(move_in.wait_send)
    pl.when(jnp.logical_not(z_self))(move_z.wait_send)

    for name in PLAN:
        w_copy(name).wait_send()
    s_copy(None, k).wait_send()
    for name in SIB:
        s_copy(name, k).wait_send()
    for b in range(2):
        for hop in range(4):
            for s in (1, -1):
                a_copy(s, hop, b).wait_send()


def per_device(
    queries, cache_keys, cache_values, span_keys, span_values, selected, counts, out_weight
):
    c = lax.axis_index("ctx")
    sel = selected.reshape(NCTX, 2, SEL)
    cnt = counts.reshape(NCTX, 2, 1)
    live = lax.broadcasted_iota(jnp.int32, sel.shape, 2) < cnt
    entry = lax.broadcasted_iota(jnp.int32, sel.shape, 1) * SEL + lax.broadcasted_iota(
        jnp.int32, sel.shape, 2
    )
    key = jnp.where(live & ((sel >> 6) == c), entry * CBLK + (sel & (CBLK - 1)), -1)
    first = jnp.min(jnp.where(key < 0, 2 * SEL * CBLK, key), axis=(1, 2))
    last = jnp.max(jnp.maximum(key, 0), axis=(1, 2))
    send = (jnp.stack((first, last), axis=1) & (CBLK - 1)).reshape(2 * NCTX)

    mine = lax.dynamic_slice_in_dim(selected, 2 * c, 2, 0)
    my_cnt = lax.dynamic_slice_in_dim(counts, 2 * c, 2, 0)
    my_live = (lax.broadcasted_iota(jnp.int32, (2, SEL), 1) < my_cnt[:, None]).reshape(2 * SEL)
    owner = (mine >> 6).reshape(2 * SEL)
    order = jnp.arange(2 * SEL, dtype=jnp.int32)
    earlier = (
        (owner[:, None] == owner[None, :]) & my_live[None, :] & (order[None, :] < order[:, None])
    )
    place = owner * 2 + jnp.any(earlier, axis=1).astype(jnp.int32)
    lead = jnp.broadcast_to(place.reshape(2, SEL)[:, :1], (2, SEL)).reshape(2 * SEL)
    place = jnp.where(my_live, place, lead)
    meta = jnp.concatenate((send, place, my_cnt))

    vmem = pltpu.VMEM
    bf16 = jnp.bfloat16
    f32 = jnp.float32
    dma = pltpu.SemaphoreType.DMA
    hbm = pl.BlockSpec(memory_space=pl.ANY)
    return pl.pallas_call(
        body,
        out_shape=jax.ShapeDtypeStruct((2 * BLK, GROUP * HD), bf16),
        in_specs=[pl.BlockSpec(memory_space=pltpu.SMEM)] + [hbm] * 6,
        out_specs=pl.BlockSpec(memory_space=vmem),
        scratch_shapes=[
            vmem((CBLK, BLK, HD), bf16),
            vmem((CBLK, BLK, HD), bf16),
            vmem((2 * BLK, GROUP * HD), bf16),
            vmem((2 * BLK, HD), bf16),
            vmem((2 * BLK, HD), bf16),
            vmem((NCTX, 2, 2, BLK, HD), bf16),
            vmem((NCTX, 2, 2, BLK, HD), bf16),
            vmem((1024, 256), bf16),
            vmem((NZ, 4, 1024, 256), bf16),
            vmem((NZ, 2, BLK, GROUP * HD), bf16),
            vmem((GROUP * BLK, HD), bf16),
            vmem((PAIRS, GROUP * BLK, 2 * BLK), f32),
            vmem((GROUP * BLK, BLK), f32),
            vmem((GROUP * BLK, BLK), f32),
            vmem((GROUP * BLK, BLK), f32),
            vmem((GROUP * BLK, HD), f32),
            dma((5,)),
            dma((NCTX,)),
            dma((NCTX,)),
            dma((4,)),
            dma((len(PLAN),)),
            dma((len(PLAN),)),
            dma((len(SIB) + 1,)),
            dma((len(SIB) + 1,)),
            dma((16,)),
            dma((16,)),
        ],
        compiler_params=pltpu.CompilerParams(
            collective_id=0, has_side_effects=True, vmem_limit_bytes=58 * 2**20
        ),
        cost_estimate=pl.CostEstimate(
            flops=8_000_000_000, bytes_accessed=30_000_000, transcendentals=7_000_000
        ),
        name="sparse_attention_projection",
    )(
        meta,
        queries,
        cache_keys.reshape(CBLK, BLK, HD),
        cache_values.reshape(CBLK, BLK, HD),
        span_keys,
        span_values,
        out_weight,
    )


def solution(mesh):
    placed = (
        P("ctx", "head"),
        P("ctx", "head"),
        P("ctx", "head"),
        P("ctx", "head"),
        P("ctx", "head"),
        P(),
        P(),
        P("head", "ctx"),
    )
    return jax.shard_map(
        per_device, mesh=mesh, in_specs=placed, out_specs=P("ctx", "head"), check_vma=False
    )
```

```python
import functools
import math

import jax
import jax.numpy as jnp
from jax import lax
from jax.experimental import pallas as pl
from jax.experimental.pallas import tpu as pltpu
from jax.sharding import PartitionSpec as P

HD = 128
BLK = 128
SEL = 24
GROUP = 8
NX = 4
NY = 4
NZ = 8
NCTX = 32
CBLK = 64
PAIRS = SEL // 2
MESH = pl.DeviceIdType.MESH
EXP_SCALE = math.log2(math.e) / math.sqrt(HD)

NEAR = [(1, 0), (3, 0), (0, 1), (0, 3)]
DIAG = [(1, 1), (3, 3), (1, 3), (3, 1)]
FAR = [(2, 0), (0, 2), (2, 1), (1, 2), (2, 3), (3, 2), (2, 2)]
KV_ORDER = [(a, b, k) for g in (NEAR, DIAG, FAR) for k in (0, 1) for a, b in g] + [(0, 0, 1)]


def weight_plan():
    plan = {}
    for path in ("a", "b"):
        base = 0 if path == "a" else 512

        def at(u, v, path=path):
            return (u, v) if path == "a" else (v, u)

        for s in (1, -1):
            plan[path, 1, 0, s] = (at(0, 0), base, 512, at(s, 0))
            quarter = base if s == 1 else base + 256
            plan[path, 2, 0, s] = (at(-s, 0), quarter, 256, at(s, 0))
            for u in (0, -1, 1, 2):
                plan[path, 3, u, s] = (at(u, 0), base, 512, at(0, s))
                plan[path, 4, u, s] = (at(u, -s), quarter, 256, at(0, s))
    return plan


PLAN = weight_plan()
PLAN_ID = {name: n for n, name in enumerate(PLAN)}
SIB = {}
for _path in ("a", "b"):
    for _u in range(-1, 3):
        for _v in range(-1, 3):
            SIB[_path, _u, _v] = len(SIB)


def body(
    meta, q_hbm, ck_hbm, cv_hbm, sk_hbm, sv_hbm, w_hbm, o_ref,
    kc, vc, qv, skv, svv, outgo, income_k, income_v, wtmp, wfull, attn, q8, scores, own_scores, mx, lsum, acc,
    weights, own_weights,
    load_sem, kv_send, kv_recv, perm_sem, w_send, w_recv, s_send, s_recv, a_send, a_recv,
):
    c = lax.axis_index("ctx")
    z = lax.axis_index("head")
    x = c // 8
    y = (c // 2) % 4
    k = c % 2

    loads = [
        pltpu.make_async_copy(src, dst, load_sem.at[n])
        for n, (src, dst) in enumerate(
            ((ck_hbm, kc), (cv_hbm, vc), (q_hbm, qv), (sk_hbm, skv), (sv_hbm, svv))
        )
    ]
    for cp in loads:
        cp.start()

    def ctx_at(dx, dy, dk=0):
        return ((x + dx + NX) % NX) * 8 + ((y + dy + NY) % NY) * 2 + (k + dk) % 2

    def flip(n):
        return n + 1 - 2 * (n % 2)

    def plane_of(path, across, mirrored):
        n = 4 * (across % 2) + 2 * ((across // 2 + mirrored) % 2) + mirrored
        return n if path == "a" else flip(n)

    def shift_of(path, plane):
        n = plane if path == "a" else flip(plane)
        mirrored = n % 2
        return 2 * ((n // 2 + mirrored) % 2) + n // 4, mirrored

    def piece_at(path, px, py):
        across = (px - z // 2 + NX) % NX
        mirrored = (py // 2 + z % 2) % 2
        return plane_of(path, across, mirrored), (py % 2 + mirrored) % 2

    in_plane, in_self, to_z, from_z, z_self, place = [], [], [], [], [], []
    for path in ("a", "b"):
        across, mirrored = shift_of(path, z)
        in_plane.append(((x + across) % NX) * 8 + jnp.where(mirrored == 1, 3 - y, y) * 2 + k)
        in_self.append((across == 0) & (mirrored == 0))
        sx = (x - across + NX) % NX
        sy = jnp.where(mirrored == 1, 3 - y, y)
        to_z.append(2 * sx + sy // 2)
        place.append(2 * (sy % 2) + k)
        from_z.append(piece_at(path, x, y)[0])
        z_self.append(to_z[-1] == z)

    barrier = pltpu.get_barrier_semaphore()

    def greet(i, carry):
        pl.semaphore_signal(barrier, inc=1, device_id=((c + i) % NCTX, z), device_id_type=MESH)
        return carry

    lax.fori_loop(1, NCTX, greet, 0)
    for dz in (1, NZ - 1):
        pl.semaphore_signal(barrier, inc=1, device_id=(c, (z + dz) % NZ), device_id_type=MESH)

    greeters = NCTX + 1
    for n in range(2):
        greeters = greeters + jnp.where(z_self[n], 0, 2)

        @pl.when(jnp.logical_not(z_self[n]))
        def _(n=n):
            pl.semaphore_signal(barrier, inc=1, device_id=(c, to_z[n]), device_id_type=MESH)
            pl.semaphore_signal(barrier, inc=1, device_id=(c, from_z[n]), device_id_type=MESH)

    pl.semaphore_wait(barrier, greeters)

    def slot(path, dx, dy, lane=None):
        zp, b = piece_at(path, (x + dx + NX) % NX, (y + dy + NY) % NY)
        return zp, 2 * b + (k if lane is None else lane)

    move_in, keep_in, move_z, keep_z = [], [], [], []
    for n in range(2):
        half = pl.ds(n * 512, 512)
        dst = wfull.at[z, place[n], half]
        sems = [perm_sem.at[4 * n + m] for m in range(4)]
        move_in.append(pltpu.make_async_remote_copy(
            src_ref=w_hbm.at[half], dst_ref=wtmp.at[half], send_sem=sems[0], recv_sem=sems[1],
            device_id=(in_plane[n], z), device_id_type=MESH,
        ))
        keep_in.append(pltpu.make_async_copy(w_hbm.at[half], wtmp.at[half], sems[1]))
        move_z.append(pltpu.make_async_remote_copy(
            src_ref=wtmp.at[half], dst_ref=dst, send_sem=sems[2], recv_sem=sems[3],
            device_id=(c, to_z[n]), device_id_type=MESH,
        ))
        keep_z.append(pltpu.make_async_copy(wtmp.at[half], dst, sems[3]))

    def either(flag, one, other):
        pl.when(flag)(one)
        pl.when(jnp.logical_not(flag))(other)

    for n in range(2):
        either(in_self[n], keep_in[n].start, move_in[n].start)

    income = (income_k, income_v)

    def kv_copy(part, d, source):
        return pltpu.make_async_remote_copy(
            src_ref=outgo.at[part, d], dst_ref=income[part].at[source],
            send_sem=kv_send.at[part, d], recv_sem=kv_recv.at[part, source],
            device_id=(d, z), device_id_type=MESH,
        )

    for part, cache in enumerate((kc, vc)):
        loads[part].wait()
        for dx, dy, dk in KV_ORDER:
            d = ctx_at(dx, dy, dk)
            for r in range(2):
                outgo[part, d, r] = cache[meta[2 * d + r]]
            kv_copy(part, d, c).start()
        for r in range(2):
            income[part][c, r] = cache[meta[2 * c + r]]
    for n in range(2):
        keep_in[n].wait()
        either(z_self[n], keep_z[n].start, move_z[n].start)
    loads[2].wait()
    loads[3].wait()
    loads[4].wait()

    def kv_landed(part):
        def one(i, carry):
            kv_copy(part, c, (c + i) % NCTX).wait_recv()
            return carry

        lax.fori_loop(1, NCTX, one, 0)

    def kv_sent(part):
        def one(i, carry):
            kv_copy(part, (c + i) % NCTX, c).wait_send()
            return carry

        lax.fori_loop(1, NCTX, one, 0)

    def w_copy(name):
        (dx, dy), row, rows, (tx, ty) = PLAN[name]
        zp, bk = slot(name[0], dx, dy)
        piece = wfull.at[zp, bk, pl.ds(row, rows)]
        n = PLAN_ID[name]
        return pltpu.make_async_remote_copy(
            src_ref=piece, dst_ref=piece, send_sem=w_send.at[n], recv_sem=w_recv.at[n],
            device_id=(ctx_at(tx, ty), z), device_id_type=MESH,
        )

    def w_arrived(name):
        (dx, dy), row, rows, (tx, ty) = PLAN[name]
        zp, bk = slot(name[0], dx - tx, dy - ty)
        piece = wfull.at[zp, bk, pl.ds(row, rows)]
        n = PLAN_ID[name]
        pltpu.make_async_remote_copy(
            src_ref=piece, dst_ref=piece, send_sem=w_send.at[n], recv_sem=w_recv.at[n],
            device_id=(ctx_at(tx, ty), z), device_id_type=MESH,
        ).wait_recv()

    def s_copy(name, lane):
        path, u, v = name
        n, row, rows = SIB[name], (0 if path == "a" else 512), 512
        zp, bk = slot(path, u, v, lane)
        piece = wfull.at[zp, bk, pl.ds(row, rows)]
        return pltpu.make_async_remote_copy(
            src_ref=piece, dst_ref=piece, send_sem=s_send.at[n], recv_sem=s_recv.at[n],
            device_id=(ctx_at(0, 0, 1), z), device_id_type=MESH,
        )

    def s_start(path, u, v):
        name = (path, u, v) if path == "a" else (path, v, u)
        s_copy(name, k).start()

    def a_ref(s, hop, b, sending):
        off = -s * hop if sending else -s * (hop + 1)
        src = attn.at[(z + off + 2 * NZ) % NZ, b]
        if hop == 3:
            src = src.at[pl.ds(0 if s == 1 else 64, 64)]
        return src

    def a_copy(s, hop, b, sending=True):
        n = (b * 4 + hop) * 2 + (0 if s == 1 else 1)
        ref = a_ref(s, hop, b, sending)
        return pltpu.make_async_remote_copy(
            src_ref=ref, dst_ref=ref, send_sem=a_send.at[n], recv_sem=a_recv.at[n],
            device_id=(c, (z + s + NZ) % NZ), device_id_type=MESH,
        )

    def a_start(hop, b):
        for s in (1, -1):
            if hop:
                a_copy(s, hop - 1, b, False).wait_recv()
            a_copy(s, hop, b).start()

    def w_own():
        for n, path in enumerate(("a", "b")):
            zp, bk = slot(path, 0, 0)
            half = pl.ds(n * 512, 512)
            pltpu.make_async_copy(wtmp.at[half], wfull.at[zp, bk, half], perm_sem.at[4 * n + 3]).wait()
        for stage in (1, 3):
            for s in (1, -1):
                for path in ("a", "b"):
                    w_copy((path, stage, 0, s)).start()
        for path in ("a", "b"):
            s_start(path, 0, 0)

    causal = lax.broadcasted_iota(jnp.int32, (BLK, BLK), 1) <= lax.broadcasted_iota(
        jnp.int32, (BLK, BLK), 0
    )
    nt = (((1,), (1,)), ((), ()))

    def weigh(b):
        for h in range(GROUP):
            q8[pl.ds(h * BLK, BLK), :] = qv[pl.ds(b * BLK, BLK), pl.ds(h * HD, HD)]
        own_k = skv[pl.ds(b * BLK, BLK), :]
        live = meta[2 * NCTX + 2 * SEL + b]
        for part in range(2):
            heads = [(h, pl.ds(h * BLK, BLK), pl.ds((part * 4 + h) * BLK, BLK)) for h in range(4)]
            for h, rows, all_rows in heads:
                s_own = lax.dot_general(
                    q8[all_rows, :], own_k, nt, preferred_element_type=jnp.float32
                )
                s_own = jnp.where(causal, s_own, -jnp.inf)
                own_scores[rows, :] = s_own
                mx[rows, :] = s_own

            def score_pair(p, carry, heads=heads):
                i0 = meta[2 * NCTX + b * SEL + 2 * p]
                i1 = meta[2 * NCTX + b * SEL + 2 * p + 1]
                keys = jnp.concatenate(
                    [income_k[i0 // 2, i0 % 2], income_k[i1 // 2, i1 % 2]], axis=0
                )
                for h, rows, all_rows in heads:
                    s = lax.dot_general(
                        q8[all_rows, :], keys, nt, preferred_element_type=jnp.float32
                    )
                    scores[p, rows, :] = s
                    mx[rows, :] = jnp.maximum(mx[rows, :], jnp.maximum(s[:, :BLK], s[:, BLK:]))
                return carry

            lax.fori_loop(0, PAIRS, score_pair, 0)

            for h, rows, all_rows in heads:
                top = jnp.max(mx[rows, :], axis=1, keepdims=True) * EXP_SCALE
                top = jnp.broadcast_to(top, (BLK, BLK))
                mx[rows, :] = top
                w = jnp.exp2(own_scores[rows, :] * EXP_SCALE - top)
                lsum[b, all_rows, :] = w
                own_weights[b, all_rows, :] = w.astype(jnp.bfloat16)

            def weight_pair(p, carry, heads=heads):
                off0 = jnp.where(2 * p < live, 0.0, 1e30).astype(jnp.float32)
                off1 = jnp.where(2 * p + 1 < live, 0.0, 1e30).astype(jnp.float32)
                for h, rows, all_rows in heads:
                    top = mx[rows, :]
                    s = scores[p, rows, :]
                    w0 = jnp.exp2(s[:, :BLK] * EXP_SCALE - (top + off0))
                    w1 = jnp.exp2(s[:, BLK:] * EXP_SCALE - (top + off1))
                    lsum[b, all_rows, :] = lsum[b, all_rows, :] + (w0 + w1)
                    weights[b, p, all_rows, :BLK] = w0.astype(jnp.bfloat16)
                    weights[b, p, all_rows, BLK:] = w1.astype(jnp.bfloat16)
                return carry

            lax.fori_loop(0, PAIRS, weight_pair, 0)

    def apply(b):
        own_v = svv[pl.ds(b * BLK, BLK), :]
        for h in range(GROUP):
            rows = pl.ds(h * BLK, BLK)
            acc[rows, :] = jnp.dot(
                own_weights[b, rows, :], own_v, preferred_element_type=jnp.float32
            )

        def value_pairs(t, carry):
            vals = []
            for m in range(4):
                i0 = meta[2 * NCTX + b * SEL + 8 * t + 2 * m]
                i1 = meta[2 * NCTX + b * SEL + 8 * t + 2 * m + 1]
                vals.append(jnp.concatenate(
                    [income_v[i0 // 2, i0 % 2], income_v[i1 // 2, i1 % 2]], axis=0
                ))
            for h in range(GROUP):
                rows = pl.ds(h * BLK, BLK)
                total = acc[rows, :]
                for m in range(4):
                    total = total + jnp.dot(
                        weights[b, 4 * t + m, rows, :], vals[m], preferred_element_type=jnp.float32
                    )
                acc[rows, :] = total
            return carry

        lax.fori_loop(0, PAIRS // 4, value_pairs, 0)
        for h in range(GROUP):
            rows = pl.ds(h * BLK, BLK)
            total = jnp.sum(lsum[b, rows, :], axis=1, keepdims=True)
            attn[z, b, :, pl.ds(h * HD, HD)] = (acc[rows, :] / total).astype(jnp.bfloat16)

    kv_landed(0)
    weigh(0)
    w_own()
    weigh(1)
    kv_landed(1)
    apply(0)
    a_start(0, 0)

    for path in ("a", "b"):
        for s in (1, -1):
            w_arrived((path, 1, 0, s))
            w_copy((path, 2, 0, s)).start()
    for path in ("a", "b"):
        for u in (-1, 1):
            for s in (1, -1):
                w_copy((path, 3, u, s)).start()
            s_start(path, u, 0)

    apply(1)
    a_start(0, 1)
    a_start(1, 0)

    def w_far():
        for path in ("a", "b"):
            for s in (1, -1):
                w_arrived((path, 2, 0, s))
        for path in ("a", "b"):
            for s in (1, -1):
                w_copy((path, 3, 2, s)).start()
            s_start(path, 2, 0)

    def w_pass(u):
        for path in ("a", "b"):
            for s in (1, -1):
                w_arrived((path, 3, u, s))
                w_copy((path, 4, u, s)).start()
                s_start(path, u, -s)

    w_pass(0)
    w_far()
    a_start(1, 1)
    a_start(2, 0)
    w_pass(-1)
    a_start(2, 1)
    w_pass(1)
    a_start(3, 0)
    w_pass(2)
    a_start(3, 1)
    for u in (0, -1, 1, 2):
        for path in ("a", "b"):
            for s in (1, -1):
                w_arrived((path, 4, u, s))
            s_start(path, u, 2)

    for name in SIB:
        s_copy(name, 1 - k).wait_recv()
    for b in range(2):
        for s in (1, -1):
            a_copy(s, 3, b, False).wait_recv()

    for bk in range(4):
        total = jnp.zeros((2 * BLK, 256), jnp.float32)
        for zp in range(NZ):
            total = total + jnp.dot(
                attn[zp].reshape(2 * BLK, GROUP * HD), wfull[zp, bk],
                preferred_element_type=jnp.float32,
            )
        o_ref[:, pl.ds(bk * 256, 256)] = total.astype(jnp.bfloat16)

    for n in range(2):
        pl.when(jnp.logical_not(in_self[n]))(move_in[n].wait_send)
        pl.when(jnp.logical_not(z_self[n]))(move_z[n].wait_send)
    kv_sent(0)
    kv_sent(1)

    for name in PLAN:
        w_copy(name).wait_send()
    for name in SIB:
        s_copy(name, k).wait_send()
    for b in range(2):
        for hop in range(4):
            for s in (1, -1):
                a_copy(s, hop, b).wait_send()


def per_device(
    queries, cache_keys, cache_values, span_keys, span_values, selected, counts, out_weight
):
    c = lax.axis_index("ctx")
    sel = selected.reshape(NCTX, 2, SEL)
    cnt = counts.reshape(NCTX, 2, 1)
    live = lax.broadcasted_iota(jnp.int32, sel.shape, 2) < cnt
    entry = lax.broadcasted_iota(jnp.int32, sel.shape, 1) * SEL + lax.broadcasted_iota(
        jnp.int32, sel.shape, 2
    )
    key = jnp.where(live & ((sel >> 6) == c), entry * CBLK + (sel & (CBLK - 1)), -1)
    first = jnp.min(jnp.where(key < 0, 2 * SEL * CBLK, key), axis=(1, 2))
    last = jnp.max(jnp.maximum(key, 0), axis=(1, 2))
    send = (jnp.stack((first, last), axis=1) & (CBLK - 1)).reshape(2 * NCTX)

    mine = lax.dynamic_slice_in_dim(selected, 2 * c, 2, 0)
    my_cnt = lax.dynamic_slice_in_dim(counts, 2 * c, 2, 0)
    my_live = (lax.broadcasted_iota(jnp.int32, (2, SEL), 1) < my_cnt[:, None]).reshape(2 * SEL)
    owner = (mine >> 6).reshape(2 * SEL)
    order = jnp.arange(2 * SEL, dtype=jnp.int32)
    earlier = (
        (owner[:, None] == owner[None, :]) & my_live[None, :] & (order[None, :] < order[:, None])
    )
    place = owner * 2 + jnp.any(earlier, axis=1).astype(jnp.int32)
    lead = jnp.broadcast_to(place.reshape(2, SEL)[:, :1], (2, SEL)).reshape(2 * SEL)
    place = jnp.where(my_live, place, lead)
    meta = jnp.concatenate((send, place, my_cnt))

    vmem = pltpu.VMEM
    bf16 = jnp.bfloat16
    f32 = jnp.float32
    dma = pltpu.SemaphoreType.DMA
    hbm = pl.BlockSpec(memory_space=pl.ANY)
    return pl.pallas_call(
        body,
        out_shape=jax.ShapeDtypeStruct((2 * BLK, GROUP * HD), bf16),
        in_specs=[pl.BlockSpec(memory_space=pltpu.SMEM)] + [hbm] * 6,
        out_specs=pl.BlockSpec(memory_space=vmem),
        scratch_shapes=[
            vmem((CBLK, BLK, HD), bf16),
            vmem((CBLK, BLK, HD), bf16),
            vmem((2 * BLK, GROUP * HD), bf16),
            vmem((2 * BLK, HD), bf16),
            vmem((2 * BLK, HD), bf16),
            vmem((2, NCTX, 2, BLK, HD), bf16),
            vmem((NCTX, 2, BLK, HD), bf16),
            vmem((NCTX, 2, BLK, HD), bf16),
            vmem((1024, 256), bf16),
            vmem((NZ, 4, 1024, 256), bf16),
            vmem((NZ, 2, BLK, GROUP * HD), bf16),
            vmem((GROUP * BLK, HD), bf16),
            vmem((PAIRS, 4 * BLK, 2 * BLK), f32),
            vmem((4 * BLK, BLK), f32),
            vmem((4 * BLK, BLK), f32),
            vmem((2, GROUP * BLK, BLK), f32),
            vmem((GROUP * BLK, HD), f32),
            vmem((2, PAIRS, GROUP * BLK, 2 * BLK), bf16),
            vmem((2, GROUP * BLK, BLK), bf16),
            dma((5,)),
            dma((2, NCTX)),
            dma((2, NCTX)),
            dma((8,)),
            dma((len(PLAN),)),
            dma((len(PLAN),)),
            dma((len(SIB),)),
            dma((len(SIB),)),
            dma((16,)),
            dma((16,)),
        ],
        compiler_params=pltpu.CompilerParams(
            collective_id=0, has_side_effects=True, vmem_limit_bytes=58 * 2**20
        ),
        cost_estimate=pl.CostEstimate(
            flops=8_000_000_000, bytes_accessed=30_000_000, transcendentals=7_000_000
        ),
        name="sparse_attention_projection",
    )(
        meta,
        queries,
        cache_keys.reshape(CBLK, BLK, HD),
        cache_values.reshape(CBLK, BLK, HD),
        span_keys,
        span_values,
        out_weight,
    )


def solution(mesh):
    placed = (
        P("ctx", "head"),
        P("ctx", "head"),
        P("ctx", "head"),
        P("ctx", "head"),
        P("ctx", "head"),
        P(),
        P(),
        P("head", "ctx"),
    )
    return jax.shard_map(
        per_device, mesh=mesh, in_specs=placed, out_specs=P("ctx", "head"), check_vma=False
    )
```

```python
import functools
import math

import jax
import jax.numpy as jnp
from jax import lax
from jax.experimental import pallas as pl
from jax.experimental.pallas import tpu as pltpu
from jax.sharding import PartitionSpec as P

HD = 128
BLK = 128
SEL = 24
GROUP = 8
NX = 4
NY = 4
NZ = 8
NCTX = 32
CBLK = 64
PAIRS = SEL // 2
UNROLL = 3
MESH = pl.DeviceIdType.MESH
EXP_SCALE = math.log2(math.e) / math.sqrt(HD)

NEAR = [(1, 0), (3, 0), (0, 1), (0, 3)]
DIAG = [(1, 1), (3, 3), (1, 3), (3, 1)]
FAR = [(2, 0), (0, 2), (2, 1), (1, 2), (2, 3), (3, 2), (2, 2)]
KV_ORDER = [(a, b, k) for g in (NEAR, DIAG, FAR) for k in (0, 1) for a, b in g] + [(0, 0, 1)]


def weight_plan():
    plan = {}
    for path in ("a", "b"):
        base = 0 if path == "a" else 512

        def at(u, v, path=path):
            return (u, v) if path == "a" else (v, u)

        for s in (1, -1):
            plan[path, 1, 0, s] = (at(0, 0), base, 512, at(s, 0))
            quarter = base if s == 1 else base + 256
            plan[path, 2, 0, s] = (at(-s, 0), quarter, 256, at(s, 0))
            for u in (0, -1, 1, 2):
                plan[path, 3, u, s] = (at(u, 0), base, 512, at(0, s))
                plan[path, 4, u, s] = (at(u, -s), quarter, 256, at(0, s))
    return plan


PLAN = weight_plan()
PLAN_ID = {name: n for n, name in enumerate(PLAN)}
SIB = {}
for _path in ("a", "b"):
    for _u in range(-1, 3):
        for _v in range(-1, 3):
            SIB[_path, _u, _v] = len(SIB)


def body(
    meta, q_hbm, ck_hbm, cv_hbm, sk_hbm, sv_hbm, w_hbm, o_ref,
    kc, vc, qv, skv, svv, outgo, income_k, income_v, wtmp, wfull, attn, q8, scores, own_scores, mx, lsum, acc,
    weights, own_weights,
    load_sem, kv_send, kv_recv, perm_sem, w_send, w_recv, s_send, s_recv, a_send, a_recv,
):
    c = lax.axis_index("ctx")
    z = lax.axis_index("head")
    x = c // 8
    y = (c // 2) % 4
    k = c % 2

    loads = [
        pltpu.make_async_copy(src, dst, load_sem.at[n])
        for n, (src, dst) in enumerate(
            ((ck_hbm, kc), (cv_hbm, vc), (q_hbm, qv), (sk_hbm, skv), (sv_hbm, svv))
        )
    ]
    for cp in loads:
        cp.start()

    def ctx_at(dx, dy, dk=0):
        return ((x + dx + NX) % NX) * 8 + ((y + dy + NY) % NY) * 2 + (k + dk) % 2

    def flip(n):
        return n + 1 - 2 * (n % 2)

    def table(n, values):
        return sum(jnp.where(n == m, v, 0) for m, v in enumerate(values))

    def plane_of(path, across, mirrored):
        n = 4 * (across % 2) + 2 * ((across // 2 + mirrored) % 2) + mirrored
        return table(n if path == "a" else flip(n), (0, 1, 7, 4, 2, 5, 3, 6))

    def shift_of(path, plane):
        n = table(plane, (0, 1, 4, 6, 3, 5, 7, 2))
        n = n if path == "a" else flip(n)
        mirrored = n % 2
        return 2 * ((n // 2 + mirrored) % 2) + n // 4, mirrored

    def piece_at(path, px, py):
        across = (px - z // 2 + NX) % NX
        mirrored = (py // 2 + z % 2) % 2
        return plane_of(path, across, mirrored), (py % 2 + mirrored) % 2

    in_plane, in_self, to_z, from_z, z_self, place = [], [], [], [], [], []
    for path in ("a", "b"):
        across, mirrored = shift_of(path, z)
        in_plane.append(((x + across) % NX) * 8 + jnp.where(mirrored == 1, 3 - y, y) * 2 + k)
        in_self.append((across == 0) & (mirrored == 0))
        sx = (x - across + NX) % NX
        sy = jnp.where(mirrored == 1, 3 - y, y)
        to_z.append(2 * sx + sy // 2)
        place.append(2 * (sy % 2) + k)
        from_z.append(piece_at(path, x, y)[0])
        z_self.append(to_z[-1] == z)

    barrier = pltpu.get_barrier_semaphore()

    def greet(i, carry):
        pl.semaphore_signal(barrier, inc=1, device_id=((c + i) % NCTX, z), device_id_type=MESH)
        return carry

    lax.fori_loop(1, NCTX, greet, 0)
    for dz in (1, NZ - 1):
        pl.semaphore_signal(barrier, inc=1, device_id=(c, (z + dz) % NZ), device_id_type=MESH)

    greeters = NCTX + 1
    for n in range(2):
        greeters = greeters + jnp.where(z_self[n], 0, 2)

        @pl.when(jnp.logical_not(z_self[n]))
        def _(n=n):
            pl.semaphore_signal(barrier, inc=1, device_id=(c, to_z[n]), device_id_type=MESH)
            pl.semaphore_signal(barrier, inc=1, device_id=(c, from_z[n]), device_id_type=MESH)

    pl.semaphore_wait(barrier, greeters)

    def slot(path, dx, dy, lane=None):
        zp, b = piece_at(path, (x + dx + NX) % NX, (y + dy + NY) % NY)
        return zp, 2 * b + (k if lane is None else lane)

    move_in, keep_in, move_z, keep_z = [], [], [], []
    for n in range(2):
        half = pl.ds(n * 512, 512)
        dst = wfull.at[z, place[n], half]
        sems = [perm_sem.at[4 * n + m] for m in range(4)]
        move_in.append(pltpu.make_async_remote_copy(
            src_ref=w_hbm.at[half], dst_ref=wtmp.at[half], send_sem=sems[0], recv_sem=sems[1],
            device_id=(in_plane[n], z), device_id_type=MESH,
        ))
        keep_in.append(pltpu.make_async_copy(w_hbm.at[half], wtmp.at[half], sems[1]))
        move_z.append(pltpu.make_async_remote_copy(
            src_ref=wtmp.at[half], dst_ref=dst, send_sem=sems[2], recv_sem=sems[3],
            device_id=(c, to_z[n]), device_id_type=MESH,
        ))
        keep_z.append(pltpu.make_async_copy(wtmp.at[half], dst, sems[3]))

    def either(flag, one, other):
        pl.when(flag)(one)
        pl.when(jnp.logical_not(flag))(other)

    for n in range(2):
        either(in_self[n], keep_in[n].start, move_in[n].start)

    income = (income_k, income_v)

    def kv_copy(part, d, source):
        return pltpu.make_async_remote_copy(
            src_ref=outgo.at[part, d], dst_ref=income[part].at[source],
            send_sem=kv_send.at[part, d], recv_sem=kv_recv.at[part, source],
            device_id=(d, z), device_id_type=MESH,
        )

    for part, cache in enumerate((kc, vc)):
        loads[part].wait()
        for dx, dy, dk in KV_ORDER:
            d = ctx_at(dx, dy, dk)
            for r in range(2):
                outgo[part, d, r] = cache[meta[2 * d + r]]
            kv_copy(part, d, c).start()
        for r in range(2):
            income[part][c, r] = cache[meta[2 * c + r]]
    for n in range(2):
        keep_in[n].wait()
        either(z_self[n], keep_z[n].start, move_z[n].start)
    loads[2].wait()
    loads[3].wait()
    loads[4].wait()

    def kv_landed(part):
        def one(i, carry):
            kv_copy(part, c, (c + i) % NCTX).wait_recv()
            return carry

        lax.fori_loop(1, NCTX, one, 0)

    def kv_sent(part):
        def one(i, carry):
            kv_copy(part, (c + i) % NCTX, c).wait_send()
            return carry

        lax.fori_loop(1, NCTX, one, 0)

    def w_copy(name):
        (dx, dy), row, rows, (tx, ty) = PLAN[name]
        zp, bk = slot(name[0], dx, dy)
        piece = wfull.at[zp, bk, pl.ds(row, rows)]
        n = PLAN_ID[name]
        return pltpu.make_async_remote_copy(
            src_ref=piece, dst_ref=piece, send_sem=w_send.at[n], recv_sem=w_recv.at[n],
            device_id=(ctx_at(tx, ty), z), device_id_type=MESH,
        )

    def w_arrived(name):
        (dx, dy), row, rows, (tx, ty) = PLAN[name]
        zp, bk = slot(name[0], dx - tx, dy - ty)
        piece = wfull.at[zp, bk, pl.ds(row, rows)]
        n = PLAN_ID[name]
        pltpu.make_async_remote_copy(
            src_ref=piece, dst_ref=piece, send_sem=w_send.at[n], recv_sem=w_recv.at[n],
            device_id=(ctx_at(tx, ty), z), device_id_type=MESH,
        ).wait_recv()

    def s_copy(name, lane):
        path, u, v = name
        n, row, rows = SIB[name], (0 if path == "a" else 512), 512
        zp, bk = slot(path, u, v, lane)
        piece = wfull.at[zp, bk, pl.ds(row, rows)]
        return pltpu.make_async_remote_copy(
            src_ref=piece, dst_ref=piece, send_sem=s_send.at[n], recv_sem=s_recv.at[n],
            device_id=(ctx_at(0, 0, 1), z), device_id_type=MESH,
        )

    def s_start(path, u, v):
        name = (path, u, v) if path == "a" else (path, v, u)
        s_copy(name, k).start()

    def a_ref(s, hop, b, sending):
        off = -s * hop if sending else -s * (hop + 1)
        src = attn.at[(z + off + 2 * NZ) % NZ, b]
        if hop == 3:
            src = src.at[pl.ds(0 if s == 1 else 64, 64)]
        return src

    def a_copy(s, hop, b, sending=True):
        n = (b * 4 + hop) * 2 + (0 if s == 1 else 1)
        ref = a_ref(s, hop, b, sending)
        return pltpu.make_async_remote_copy(
            src_ref=ref, dst_ref=ref, send_sem=a_send.at[n], recv_sem=a_recv.at[n],
            device_id=(c, (z + s + NZ) % NZ), device_id_type=MESH,
        )

    def a_start(hop, b):
        for s in (1, -1):
            if hop:
                a_copy(s, hop - 1, b, False).wait_recv()
            a_copy(s, hop, b).start()

    def w_own():
        for n, path in enumerate(("a", "b")):
            zp, bk = slot(path, 0, 0)
            half = pl.ds(n * 512, 512)
            pltpu.make_async_copy(wtmp.at[half], wfull.at[zp, bk, half], perm_sem.at[4 * n + 3]).wait()
        for stage in (1, 3):
            for s in (1, -1):
                for path in ("a", "b"):
                    w_copy((path, stage, 0, s)).start()
        for path in ("a", "b"):
            s_start(path, 0, 0)

    causal = lax.broadcasted_iota(jnp.int32, (BLK, BLK), 1) <= lax.broadcasted_iota(
        jnp.int32, (BLK, BLK), 0
    )
    nt = (((1,), (1,)), ((), ()))

    def weigh(b):
        for h in range(GROUP):
            q8[pl.ds(h * BLK, BLK), :] = qv[pl.ds(b * BLK, BLK), pl.ds(h * HD, HD)]
        own_k = skv[pl.ds(b * BLK, BLK), :]
        live = meta[2 * NCTX + 2 * SEL + b]
        for part in range(2):
            heads = [(h, pl.ds(h * BLK, BLK), pl.ds((part * 4 + h) * BLK, BLK)) for h in range(4)]
            for h, rows, all_rows in heads:
                s_own = lax.dot_general(
                    q8[all_rows, :], own_k, nt, preferred_element_type=jnp.float32
                )
                s_own = jnp.where(causal, s_own, -jnp.inf)
                own_scores[rows, :] = s_own
                mx[rows, :] = s_own

            def score_pairs(t, carry, heads=heads):
                keys = []
                for m in range(UNROLL):
                    i0 = meta[2 * NCTX + b * SEL + 2 * (UNROLL * t + m)]
                    i1 = meta[2 * NCTX + b * SEL + 2 * (UNROLL * t + m) + 1]
                    keys.append(jnp.concatenate(
                        [income_k[i0 // 2, i0 % 2], income_k[i1 // 2, i1 % 2]], axis=0
                    ))
                for h, rows, all_rows in heads:
                    top = mx[rows, :]
                    for m in range(UNROLL):
                        s = lax.dot_general(
                            q8[all_rows, :], keys[m], nt, preferred_element_type=jnp.float32
                        )
                        scores[UNROLL * t + m, rows, :] = s
                        top = jnp.maximum(top, jnp.maximum(s[:, :BLK], s[:, BLK:]))
                    mx[rows, :] = top
                return carry

            lax.fori_loop(0, PAIRS // UNROLL, score_pairs, 0)

            for h, rows, all_rows in heads:
                top = jnp.max(mx[rows, :], axis=1, keepdims=True) * EXP_SCALE
                top = jnp.broadcast_to(top, (BLK, BLK))
                mx[rows, :] = top
                w = jnp.exp2(own_scores[rows, :] * EXP_SCALE - top)
                lsum[b, all_rows, :] = w
                own_weights[b, all_rows, :] = w.astype(jnp.bfloat16)

            def weight_pairs(t, carry, heads=heads):
                for h, rows, all_rows in heads:
                    top = mx[rows, :]
                    total = lsum[b, all_rows, :]
                    for m in range(UNROLL):
                        p = UNROLL * t + m
                        off0 = jnp.where(2 * p < live, 0.0, 1e30).astype(jnp.float32)
                        off1 = jnp.where(2 * p + 1 < live, 0.0, 1e30).astype(jnp.float32)
                        s = scores[p, rows, :]
                        w0 = jnp.exp2(s[:, :BLK] * EXP_SCALE - (top + off0))
                        w1 = jnp.exp2(s[:, BLK:] * EXP_SCALE - (top + off1))
                        total = total + (w0 + w1)
                        weights[b, p, all_rows, :BLK] = w0.astype(jnp.bfloat16)
                        weights[b, p, all_rows, BLK:] = w1.astype(jnp.bfloat16)
                    lsum[b, all_rows, :] = total
                return carry

            lax.fori_loop(0, PAIRS // UNROLL, weight_pairs, 0)

    def apply(b):
        own_v = svv[pl.ds(b * BLK, BLK), :]
        for h in range(GROUP):
            rows = pl.ds(h * BLK, BLK)
            acc[rows, :] = jnp.dot(
                own_weights[b, rows, :], own_v, preferred_element_type=jnp.float32
            )

        def value_pairs(t, carry):
            vals = []
            for m in range(4):
                i0 = meta[2 * NCTX + b * SEL + 8 * t + 2 * m]
                i1 = meta[2 * NCTX + b * SEL + 8 * t + 2 * m + 1]
                vals.append(jnp.concatenate(
                    [income_v[i0 // 2, i0 % 2], income_v[i1 // 2, i1 % 2]], axis=0
                ))
            for h in range(GROUP):
                rows = pl.ds(h * BLK, BLK)
                total = acc[rows, :]
                for m in range(4):
                    total = total + jnp.dot(
                        weights[b, 4 * t + m, rows, :], vals[m], preferred_element_type=jnp.float32
                    )
                acc[rows, :] = total
            return carry

        lax.fori_loop(0, PAIRS // 4, value_pairs, 0)
        for h in range(GROUP):
            rows = pl.ds(h * BLK, BLK)
            total = jnp.sum(lsum[b, rows, :], axis=1, keepdims=True)
            attn[z, b, :, pl.ds(h * HD, HD)] = (acc[rows, :] / total).astype(jnp.bfloat16)

    kv_landed(0)
    weigh(0)
    w_own()
    weigh(1)
    kv_landed(1)
    apply(0)
    a_start(0, 0)

    for path in ("a", "b"):
        for s in (1, -1):
            w_arrived((path, 1, 0, s))
            w_copy((path, 2, 0, s)).start()
    for path in ("a", "b"):
        for u in (-1, 1):
            for s in (1, -1):
                w_copy((path, 3, u, s)).start()
            s_start(path, u, 0)

    apply(1)
    a_start(0, 1)
    a_start(1, 0)

    def w_far():
        for path in ("a", "b"):
            for s in (1, -1):
                w_arrived((path, 2, 0, s))
        for path in ("a", "b"):
            for s in (1, -1):
                w_copy((path, 3, 2, s)).start()
            s_start(path, 2, 0)

    def w_pass(u):
        for path in ("a", "b"):
            for s in (1, -1):
                w_arrived((path, 3, u, s))
                w_copy((path, 4, u, s)).start()
                s_start(path, u, -s)

    w_pass(0)
    w_far()
    a_start(1, 1)
    a_start(2, 0)
    w_pass(-1)
    a_start(2, 1)
    w_pass(1)
    a_start(3, 0)
    w_pass(2)
    a_start(3, 1)
    for u in (0, -1, 1, 2):
        for path in ("a", "b"):
            for s in (1, -1):
                w_arrived((path, 4, u, s))
            s_start(path, u, 2)

    for name in SIB:
        s_copy(name, 1 - k).wait_recv()
    for bk in range(4):
        total = jnp.zeros((2 * BLK, 256), jnp.float32)
        for off in (0, 1, 7, 2, 6, 3, 5):
            zp = (z + off) % NZ
            total = total + jnp.dot(
                attn[zp].reshape(2 * BLK, GROUP * HD), wfull[zp, bk],
                preferred_element_type=jnp.float32,
            )
        scores[bk, : 2 * BLK, :] = total
    for b in range(2):
        for s in (1, -1):
            a_copy(s, 3, b, False).wait_recv()
    far = (z + NZ // 2) % NZ
    for bk in range(4):
        total = scores[bk, : 2 * BLK, :] + jnp.dot(
            attn[far].reshape(2 * BLK, GROUP * HD), wfull[far, bk],
            preferred_element_type=jnp.float32,
        )
        o_ref[:, pl.ds(bk * 256, 256)] = total.astype(jnp.bfloat16)

    for n in range(2):
        pl.when(jnp.logical_not(in_self[n]))(move_in[n].wait_send)
        pl.when(jnp.logical_not(z_self[n]))(move_z[n].wait_send)
    kv_sent(0)
    kv_sent(1)

    for name in PLAN:
        w_copy(name).wait_send()
    for name in SIB:
        s_copy(name, k).wait_send()
    for b in range(2):
        for hop in range(4):
            for s in (1, -1):
                a_copy(s, hop, b).wait_send()


def per_device(
    queries, cache_keys, cache_values, span_keys, span_values, selected, counts, out_weight
):
    c = lax.axis_index("ctx")
    sel = selected.reshape(NCTX, 2, SEL)
    cnt = counts.reshape(NCTX, 2, 1)
    live = lax.broadcasted_iota(jnp.int32, sel.shape, 2) < cnt
    entry = lax.broadcasted_iota(jnp.int32, sel.shape, 1) * SEL + lax.broadcasted_iota(
        jnp.int32, sel.shape, 2
    )
    key = jnp.where(live & ((sel >> 6) == c), entry * CBLK + (sel & (CBLK - 1)), -1)
    first = jnp.min(jnp.where(key < 0, 2 * SEL * CBLK, key), axis=(1, 2))
    last = jnp.max(jnp.maximum(key, 0), axis=(1, 2))
    send = (jnp.stack((first, last), axis=1) & (CBLK - 1)).reshape(2 * NCTX)

    mine = lax.dynamic_slice_in_dim(selected, 2 * c, 2, 0)
    my_cnt = lax.dynamic_slice_in_dim(counts, 2 * c, 2, 0)
    my_live = (lax.broadcasted_iota(jnp.int32, (2, SEL), 1) < my_cnt[:, None]).reshape(2 * SEL)
    owner = (mine >> 6).reshape(2 * SEL)
    order = jnp.arange(2 * SEL, dtype=jnp.int32)
    earlier = (
        (owner[:, None] == owner[None, :]) & my_live[None, :] & (order[None, :] < order[:, None])
    )
    place = owner * 2 + jnp.any(earlier, axis=1).astype(jnp.int32)
    lead = jnp.broadcast_to(place.reshape(2, SEL)[:, :1], (2, SEL)).reshape(2 * SEL)
    place = jnp.where(my_live, place, lead)
    meta = jnp.concatenate((send, place, my_cnt))

    vmem = pltpu.VMEM
    bf16 = jnp.bfloat16
    f32 = jnp.float32
    dma = pltpu.SemaphoreType.DMA
    hbm = pl.BlockSpec(memory_space=pl.ANY)
    return pl.pallas_call(
        body,
        out_shape=jax.ShapeDtypeStruct((2 * BLK, GROUP * HD), bf16),
        in_specs=[pl.BlockSpec(memory_space=pltpu.SMEM)] + [hbm] * 6,
        out_specs=pl.BlockSpec(memory_space=vmem),
        scratch_shapes=[
            vmem((CBLK, BLK, HD), bf16),
            vmem((CBLK, BLK, HD), bf16),
            vmem((2 * BLK, GROUP * HD), bf16),
            vmem((2 * BLK, HD), bf16),
            vmem((2 * BLK, HD), bf16),
            vmem((2, NCTX, 2, BLK, HD), bf16),
            vmem((NCTX, 2, BLK, HD), bf16),
            vmem((NCTX, 2, BLK, HD), bf16),
            vmem((1024, 256), bf16),
            vmem((NZ, 4, 1024, 256), bf16),
            vmem((NZ, 2, BLK, GROUP * HD), bf16),
            vmem((GROUP * BLK, HD), bf16),
            vmem((PAIRS, 4 * BLK, 2 * BLK), f32),
            vmem((4 * BLK, BLK), f32),
            vmem((4 * BLK, BLK), f32),
            vmem((2, GROUP * BLK, BLK), f32),
            vmem((GROUP * BLK, HD), f32),
            vmem((2, PAIRS, GROUP * BLK, 2 * BLK), bf16),
            vmem((2, GROUP * BLK, BLK), bf16),
            dma((5,)),
            dma((2, NCTX)),
            dma((2, NCTX)),
            dma((8,)),
            dma((len(PLAN),)),
            dma((len(PLAN),)),
            dma((len(SIB),)),
            dma((len(SIB),)),
            dma((16,)),
            dma((16,)),
        ],
        compiler_params=pltpu.CompilerParams(
            collective_id=0, has_side_effects=True, vmem_limit_bytes=58 * 2**20
        ),
        cost_estimate=pl.CostEstimate(
            flops=8_000_000_000, bytes_accessed=30_000_000, transcendentals=7_000_000
        ),
        name="sparse_attention_projection",
    )(
        meta,
        queries,
        cache_keys.reshape(CBLK, BLK, HD),
        cache_values.reshape(CBLK, BLK, HD),
        span_keys,
        span_values,
        out_weight,
    )


def solution(mesh):
    placed = (
        P("ctx", "head"),
        P("ctx", "head"),
        P("ctx", "head"),
        P("ctx", "head"),
        P("ctx", "head"),
        P(),
        P(),
        P("head", "ctx"),
    )
    return jax.shard_map(
        per_device, mesh=mesh, in_specs=placed, out_specs=P("ctx", "head"), check_vma=False
    )
```

```python
import functools
import math

import jax
import jax.numpy as jnp
from jax import lax
from jax.experimental import pallas as pl
from jax.experimental.pallas import tpu as pltpu
from jax.sharding import PartitionSpec as P

HD = 128
BLK = 128
SEL = 24
GROUP = 8
NX = 4
NY = 4
NZ = 8
NCTX = 32
CBLK = 64
PAIRS = SEL // 2
UNROLL = 3
MESH = pl.DeviceIdType.MESH
EXP_SCALE = math.log2(math.e) / math.sqrt(HD)

NEAR = [(1, 0), (3, 0), (0, 1), (0, 3)]
DIAG = [(1, 1), (3, 3), (1, 3), (3, 1)]
FAR = [(2, 0), (0, 2), (2, 1), (1, 2), (2, 3), (3, 2), (2, 2)]
KV_ORDER = [(a, b, k) for g in (NEAR, DIAG, FAR) for k in (0, 1) for a, b in g] + [(0, 0, 1)]


def weight_plan():
    plan = {}
    for path in ("a", "b"):
        base = 0 if path == "a" else 512

        def at(u, v, path=path):
            return (u, v) if path == "a" else (v, u)

        for s in (1, -1):
            plan[path, 1, 0, s] = (at(0, 0), base, 512, at(s, 0))
            quarter = base if s == 1 else base + 256
            plan[path, 2, 0, s] = (at(-s, 0), quarter, 256, at(s, 0))
            for u in (0, -1, 1, 2):
                plan[path, 3, u, s] = (at(u, 0), base, 512, at(0, s))
                plan[path, 4, u, s] = (at(u, -s), quarter, 256, at(0, s))
    return plan


PLAN = weight_plan()
PLAN_ID = {name: n for n, name in enumerate(PLAN)}
SIB = {}
for _path in ("a", "b"):
    for _u in range(-1, 3):
        for _v in range(-1, 3):
            SIB[_path, _u, _v] = len(SIB)


def body(
    meta, q_hbm, ck_hbm, cv_hbm, sk_hbm, sv_hbm, w_hbm, o_ref,
    kc, vc, qv, skv, svv, outgo, income_k, income_v, wtmp, wfull, attn, q8, scores, own_scores, mx, lsum, acc,
    weights, own_weights,
    load_sem, kv_send, kv_recv, perm_sem, w_send, w_recv, s_send, s_recv, a_send, a_recv,
):
    c = lax.axis_index("ctx")
    z = lax.axis_index("head")
    x = c // 8
    y = (c // 2) % 4
    k = c % 2

    loads = [
        pltpu.make_async_copy(src, dst, load_sem.at[n])
        for n, (src, dst) in enumerate(
            ((ck_hbm, kc), (cv_hbm, vc), (q_hbm, qv), (sk_hbm, skv), (sv_hbm, svv))
        )
    ]
    for cp in loads:
        cp.start()

    def ctx_at(dx, dy, dk=0):
        return ((x + dx + NX) % NX) * 8 + ((y + dy + NY) % NY) * 2 + (k + dk) % 2

    def flip(n):
        return n + 1 - 2 * (n % 2)

    def table(n, values):
        return sum(jnp.where(n == m, v, 0) for m, v in enumerate(values))

    def plane_of(path, across, mirrored):
        n = 4 * (across % 2) + 2 * ((across // 2 + mirrored) % 2) + mirrored
        return table(n if path == "a" else flip(n), (0, 1, 7, 4, 2, 5, 3, 6))

    def shift_of(path, plane):
        n = table(plane, (0, 1, 4, 6, 3, 5, 7, 2))
        n = n if path == "a" else flip(n)
        mirrored = n % 2
        return 2 * ((n // 2 + mirrored) % 2) + n // 4, mirrored

    def piece_at(path, px, py):
        across = (px - z // 2 + NX) % NX
        mirrored = (py // 2 + z % 2) % 2
        return plane_of(path, across, mirrored), (py % 2 + mirrored) % 2

    in_plane, in_self, to_z, from_z, z_self, place = [], [], [], [], [], []
    for path in ("a", "b"):
        across, mirrored = shift_of(path, z)
        in_plane.append(((x + across) % NX) * 8 + jnp.where(mirrored == 1, 3 - y, y) * 2 + k)
        in_self.append((across == 0) & (mirrored == 0))
        sx = (x - across + NX) % NX
        sy = jnp.where(mirrored == 1, 3 - y, y)
        to_z.append(2 * sx + sy // 2)
        place.append(2 * (sy % 2) + k)
        from_z.append(piece_at(path, x, y)[0])
        z_self.append(to_z[-1] == z)

    barrier = pltpu.get_barrier_semaphore()

    def greet(i, carry):
        pl.semaphore_signal(barrier, inc=1, device_id=((c + i) % NCTX, z), device_id_type=MESH)
        return carry

    lax.fori_loop(1, NCTX, greet, 0)
    for dz in (1, NZ - 1):
        pl.semaphore_signal(barrier, inc=1, device_id=(c, (z + dz) % NZ), device_id_type=MESH)

    greeters = NCTX + 1
    for n in range(2):
        greeters = greeters + jnp.where(z_self[n], 0, 2)

        @pl.when(jnp.logical_not(z_self[n]))
        def _(n=n):
            pl.semaphore_signal(barrier, inc=1, device_id=(c, to_z[n]), device_id_type=MESH)
            pl.semaphore_signal(barrier, inc=1, device_id=(c, from_z[n]), device_id_type=MESH)

    pl.semaphore_wait(barrier, greeters)

    def slot(path, dx, dy, lane=None):
        zp, b = piece_at(path, (x + dx + NX) % NX, (y + dy + NY) % NY)
        return zp, 2 * b + (k if lane is None else lane)

    move_in, keep_in, move_z, keep_z = [], [], [], []
    for n in range(2):
        half = pl.ds(n * 512, 512)
        dst = wfull.at[z, place[n], half]
        sems = [perm_sem.at[4 * n + m] for m in range(4)]
        move_in.append(pltpu.make_async_remote_copy(
            src_ref=w_hbm.at[half], dst_ref=wtmp.at[half], send_sem=sems[0], recv_sem=sems[1],
            device_id=(in_plane[n], z), device_id_type=MESH,
        ))
        keep_in.append(pltpu.make_async_copy(w_hbm.at[half], wtmp.at[half], sems[1]))
        move_z.append(pltpu.make_async_remote_copy(
            src_ref=wtmp.at[half], dst_ref=dst, send_sem=sems[2], recv_sem=sems[3],
            device_id=(c, to_z[n]), device_id_type=MESH,
        ))
        keep_z.append(pltpu.make_async_copy(wtmp.at[half], dst, sems[3]))

    def either(flag, one, other):
        pl.when(flag)(one)
        pl.when(jnp.logical_not(flag))(other)

    for n in range(2):
        either(in_self[n], keep_in[n].start, move_in[n].start)

    income = (income_k, income_v)

    def kv_copy(part, d, source):
        return pltpu.make_async_remote_copy(
            src_ref=outgo.at[part, d], dst_ref=income[part].at[source],
            send_sem=kv_send.at[part, d], recv_sem=kv_recv.at[part, source],
            device_id=(d, z), device_id_type=MESH,
        )

    for part, cache in enumerate((kc, vc)):
        loads[part].wait()
        for dx, dy, dk in KV_ORDER:
            d = ctx_at(dx, dy, dk)
            for r in range(2):
                outgo[part, d, r] = cache[meta[2 * d + r]]
            kv_copy(part, d, c).start()
        for r in range(2):
            income[part][c, r] = cache[meta[2 * c + r]]
    for n in range(2):
        keep_in[n].wait()
        either(z_self[n], keep_z[n].start, move_z[n].start)
    loads[2].wait()
    loads[3].wait()
    loads[4].wait()

    def kv_landed(part):
        def one(i, carry):
            kv_copy(part, c, (c + i) % NCTX).wait_recv()
            return carry

        lax.fori_loop(1, NCTX, one, 0)

    def kv_sent(part):
        def one(i, carry):
            kv_copy(part, (c + i) % NCTX, c).wait_send()
            return carry

        lax.fori_loop(1, NCTX, one, 0)

    def w_copy(name):
        (dx, dy), row, rows, (tx, ty) = PLAN[name]
        zp, bk = slot(name[0], dx, dy)
        piece = wfull.at[zp, bk, pl.ds(row, rows)]
        n = PLAN_ID[name]
        return pltpu.make_async_remote_copy(
            src_ref=piece, dst_ref=piece, send_sem=w_send.at[n], recv_sem=w_recv.at[n],
            device_id=(ctx_at(tx, ty), z), device_id_type=MESH,
        )

    def w_arrived(name):
        (dx, dy), row, rows, (tx, ty) = PLAN[name]
        zp, bk = slot(name[0], dx - tx, dy - ty)
        piece = wfull.at[zp, bk, pl.ds(row, rows)]
        n = PLAN_ID[name]
        pltpu.make_async_remote_copy(
            src_ref=piece, dst_ref=piece, send_sem=w_send.at[n], recv_sem=w_recv.at[n],
            device_id=(ctx_at(tx, ty), z), device_id_type=MESH,
        ).wait_recv()

    def s_copy(name, lane):
        path, u, v = name
        n, row, rows = SIB[name], (0 if path == "a" else 512), 512
        zp, bk = slot(path, u, v, lane)
        piece = wfull.at[zp, bk, pl.ds(row, rows)]
        return pltpu.make_async_remote_copy(
            src_ref=piece, dst_ref=piece, send_sem=s_send.at[n], recv_sem=s_recv.at[n],
            device_id=(ctx_at(0, 0, 1), z), device_id_type=MESH,
        )

    def s_start(path, u, v):
        name = (path, u, v) if path == "a" else (path, v, u)
        s_copy(name, k).start()

    def a_ref(s, hop, b, sending):
        off = -s * hop if sending else -s * (hop + 1)
        src = attn.at[(z + off + 2 * NZ) % NZ, b]
        if hop == 3:
            src = src.at[pl.ds(0 if s == 1 else 64, 64)]
        return src

    def a_copy(s, hop, b, sending=True):
        n = (b * 4 + hop) * 2 + (0 if s == 1 else 1)
        ref = a_ref(s, hop, b, sending)
        return pltpu.make_async_remote_copy(
            src_ref=ref, dst_ref=ref, send_sem=a_send.at[n], recv_sem=a_recv.at[n],
            device_id=(c, (z + s + NZ) % NZ), device_id_type=MESH,
        )

    def a_start(hop, b):
        for s in (1, -1):
            if hop:
                a_copy(s, hop - 1, b, False).wait_recv()
            a_copy(s, hop, b).start()

    def w_own():
        for n, path in enumerate(("a", "b")):
            zp, bk = slot(path, 0, 0)
            half = pl.ds(n * 512, 512)
            pltpu.make_async_copy(wtmp.at[half], wfull.at[zp, bk, half], perm_sem.at[4 * n + 3]).wait()
        for stage in (1, 3):
            for s in (1, -1):
                for path in ("a", "b"):
                    w_copy((path, stage, 0, s)).start()
        for path in ("a", "b"):
            s_start(path, 0, 0)

    causal = lax.broadcasted_iota(jnp.int32, (BLK, BLK), 1) <= lax.broadcasted_iota(
        jnp.int32, (BLK, BLK), 0
    )
    nt = (((1,), (1,)), ((), ()))

    def weigh(b):
        for h in range(GROUP):
            q8[pl.ds(h * BLK, BLK), :] = qv[pl.ds(b * BLK, BLK), pl.ds(h * HD, HD)]
        own_k = skv[pl.ds(b * BLK, BLK), :]
        live = meta[2 * NCTX + 2 * SEL + b]
        for part in range(2):
            heads = [(h, pl.ds(h * BLK, BLK), pl.ds((part * 4 + h) * BLK, BLK)) for h in range(4)]
            for h, rows, all_rows in heads:
                s_own = lax.dot_general(
                    q8[all_rows, :], own_k, nt, preferred_element_type=jnp.float32
                )
                s_own = jnp.where(causal, s_own, -jnp.inf)
                own_scores[rows, :] = s_own
                mx[rows, :] = s_own

            def score_pairs(t, carry, heads=heads):
                keys = []
                for m in range(UNROLL):
                    i0 = meta[2 * NCTX + b * SEL + 2 * (UNROLL * t + m)]
                    i1 = meta[2 * NCTX + b * SEL + 2 * (UNROLL * t + m) + 1]
                    keys.append(jnp.concatenate(
                        [income_k[i0 // 2, i0 % 2], income_k[i1 // 2, i1 % 2]], axis=0
                    ))
                for h, rows, all_rows in heads:
                    top = mx[rows, :]
                    for m in range(UNROLL):
                        s = lax.dot_general(
                            q8[all_rows, :], keys[m], nt, preferred_element_type=jnp.float32
                        )
                        scores[UNROLL * t + m, rows, :] = s
                        top = jnp.maximum(top, jnp.maximum(s[:, :BLK], s[:, BLK:]))
                    mx[rows, :] = top
                return carry

            lax.fori_loop(0, PAIRS // UNROLL, score_pairs, 0)

            for h, rows, all_rows in heads:
                top = jnp.max(mx[rows, :], axis=1, keepdims=True) * EXP_SCALE
                top = jnp.broadcast_to(top, (BLK, BLK))
                mx[rows, :] = top
                w = jnp.exp2(own_scores[rows, :] * EXP_SCALE - top)
                lsum[b, all_rows, :] = w
                own_weights[b, all_rows, :] = w.astype(jnp.bfloat16)

            def weight_pairs(t, carry, heads=heads):
                for h, rows, all_rows in heads:
                    top = mx[rows, :]
                    total = lsum[b, all_rows, :]
                    for m in range(UNROLL):
                        p = UNROLL * t + m
                        off0 = jnp.where(2 * p < live, 0.0, 1e30).astype(jnp.float32)
                        off1 = jnp.where(2 * p + 1 < live, 0.0, 1e30).astype(jnp.float32)
                        s = scores[p, rows, :]
                        w0 = jnp.exp2(s[:, :BLK] * EXP_SCALE - (top + off0))
                        w1 = jnp.exp2(s[:, BLK:] * EXP_SCALE - (top + off1))
                        total = total + (w0 + w1)
                        weights[b, p, all_rows, :BLK] = w0.astype(jnp.bfloat16)
                        weights[b, p, all_rows, BLK:] = w1.astype(jnp.bfloat16)
                    lsum[b, all_rows, :] = total
                return carry

            lax.fori_loop(0, PAIRS // UNROLL, weight_pairs, 0)

    def apply(b):
        own_v = svv[pl.ds(b * BLK, BLK), :]
        for h in range(GROUP):
            rows = pl.ds(h * BLK, BLK)
            acc[rows, :] = jnp.dot(
                own_weights[b, rows, :], own_v, preferred_element_type=jnp.float32
            )

        def value_pairs(t, carry):
            vals = []
            for m in range(4):
                i0 = meta[2 * NCTX + b * SEL + 8 * t + 2 * m]
                i1 = meta[2 * NCTX + b * SEL + 8 * t + 2 * m + 1]
                vals.append(jnp.concatenate(
                    [income_v[i0 // 2, i0 % 2], income_v[i1 // 2, i1 % 2]], axis=0
                ))
            for h in range(GROUP):
                rows = pl.ds(h * BLK, BLK)
                total = acc[rows, :]
                for m in range(4):
                    total = total + jnp.dot(
                        weights[b, 4 * t + m, rows, :], vals[m], preferred_element_type=jnp.float32
                    )
                acc[rows, :] = total
            return carry

        lax.fori_loop(0, PAIRS // 4, value_pairs, 0)
        for h in range(GROUP):
            rows = pl.ds(h * BLK, BLK)
            total = jnp.sum(lsum[b, rows, :], axis=1, keepdims=True)
            attn[z, b, :, pl.ds(h * HD, HD)] = (acc[rows, :] / total).astype(jnp.bfloat16)

    kv_landed(0)
    weigh(0)
    w_own()
    weigh(1)
    kv_landed(1)
    apply(0)
    a_start(0, 0)
    apply(1)
    a_start(0, 1)

    for path in ("a", "b"):
        for s in (1, -1):
            w_arrived((path, 1, 0, s))
            w_copy((path, 2, 0, s)).start()
    for path in ("a", "b"):
        for u in (-1, 1):
            for s in (1, -1):
                w_copy((path, 3, u, s)).start()
            s_start(path, u, 0)

    a_start(1, 0)

    def w_far():
        for path in ("a", "b"):
            for s in (1, -1):
                w_arrived((path, 2, 0, s))
        for path in ("a", "b"):
            for s in (1, -1):
                w_copy((path, 3, 2, s)).start()
            s_start(path, 2, 0)

    def w_pass(u):
        for path in ("a", "b"):
            for s in (1, -1):
                w_arrived((path, 3, u, s))
                w_copy((path, 4, u, s)).start()
                s_start(path, u, -s)

    w_pass(0)
    w_far()
    a_start(1, 1)
    a_start(2, 0)
    w_pass(-1)
    a_start(2, 1)
    w_pass(1)
    a_start(3, 0)
    w_pass(2)
    a_start(3, 1)
    for u in (0, -1, 1, 2):
        for path in ("a", "b"):
            for s in (1, -1):
                w_arrived((path, 4, u, s))
            s_start(path, u, 2)

    for name in SIB:
        s_copy(name, 1 - k).wait_recv()
    for bk in range(4):
        total = jnp.zeros((2 * BLK, 256), jnp.float32)
        for off in (0, 1, 7, 2, 6, 3, 5):
            zp = (z + off) % NZ
            total = total + jnp.dot(
                attn[zp].reshape(2 * BLK, GROUP * HD), wfull[zp, bk],
                preferred_element_type=jnp.float32,
            )
        scores[bk, : 2 * BLK, :] = total
    for b in range(2):
        for s in (1, -1):
            a_copy(s, 3, b, False).wait_recv()
    far = (z + NZ // 2) % NZ
    for bk in range(4):
        total = scores[bk, : 2 * BLK, :] + jnp.dot(
            attn[far].reshape(2 * BLK, GROUP * HD), wfull[far, bk],
            preferred_element_type=jnp.float32,
        )
        o_ref[:, pl.ds(bk * 256, 256)] = total.astype(jnp.bfloat16)

    for n in range(2):
        pl.when(jnp.logical_not(in_self[n]))(move_in[n].wait_send)
        pl.when(jnp.logical_not(z_self[n]))(move_z[n].wait_send)
    kv_sent(0)
    kv_sent(1)

    for name in PLAN:
        w_copy(name).wait_send()
    for name in SIB:
        s_copy(name, k).wait_send()
    for b in range(2):
        for hop in range(4):
            for s in (1, -1):
                a_copy(s, hop, b).wait_send()


def per_device(
    queries, cache_keys, cache_values, span_keys, span_values, selected, counts, out_weight
):
    c = lax.axis_index("ctx")
    sel = selected.reshape(NCTX, 2, SEL)
    cnt = counts.reshape(NCTX, 2, 1)
    live = lax.broadcasted_iota(jnp.int32, sel.shape, 2) < cnt
    entry = lax.broadcasted_iota(jnp.int32, sel.shape, 1) * SEL + lax.broadcasted_iota(
        jnp.int32, sel.shape, 2
    )
    key = jnp.where(live & ((sel >> 6) == c), entry * CBLK + (sel & (CBLK - 1)), -1)
    first = jnp.min(jnp.where(key < 0, 2 * SEL * CBLK, key), axis=(1, 2))
    last = jnp.max(jnp.maximum(key, 0), axis=(1, 2))
    send = (jnp.stack((first, last), axis=1) & (CBLK - 1)).reshape(2 * NCTX)

    mine = lax.dynamic_slice_in_dim(selected, 2 * c, 2, 0)
    my_cnt = lax.dynamic_slice_in_dim(counts, 2 * c, 2, 0)
    my_live = (lax.broadcasted_iota(jnp.int32, (2, SEL), 1) < my_cnt[:, None]).reshape(2 * SEL)
    owner = (mine >> 6).reshape(2 * SEL)
    order = jnp.arange(2 * SEL, dtype=jnp.int32)
    earlier = (
        (owner[:, None] == owner[None, :]) & my_live[None, :] & (order[None, :] < order[:, None])
    )
    place = owner * 2 + jnp.any(earlier, axis=1).astype(jnp.int32)
    lead = jnp.broadcast_to(place.reshape(2, SEL)[:, :1], (2, SEL)).reshape(2 * SEL)
    place = jnp.where(my_live, place, lead)
    meta = jnp.concatenate((send, place, my_cnt))

    vmem = pltpu.VMEM
    bf16 = jnp.bfloat16
    f32 = jnp.float32
    dma = pltpu.SemaphoreType.DMA
    hbm = pl.BlockSpec(memory_space=pl.ANY)
    return pl.pallas_call(
        body,
        out_shape=jax.ShapeDtypeStruct((2 * BLK, GROUP * HD), bf16),
        in_specs=[pl.BlockSpec(memory_space=pltpu.SMEM)] + [hbm] * 6,
        out_specs=pl.BlockSpec(memory_space=vmem),
        scratch_shapes=[
            vmem((CBLK, BLK, HD), bf16),
            vmem((CBLK, BLK, HD), bf16),
            vmem((2 * BLK, GROUP * HD), bf16),
            vmem((2 * BLK, HD), bf16),
            vmem((2 * BLK, HD), bf16),
            vmem((2, NCTX, 2, BLK, HD), bf16),
            vmem((NCTX, 2, BLK, HD), bf16),
            vmem((NCTX, 2, BLK, HD), bf16),
            vmem((1024, 256), bf16),
            vmem((NZ, 4, 1024, 256), bf16),
            vmem((NZ, 2, BLK, GROUP * HD), bf16),
            vmem((GROUP * BLK, HD), bf16),
            vmem((PAIRS, 4 * BLK, 2 * BLK), f32),
            vmem((4 * BLK, BLK), f32),
            vmem((4 * BLK, BLK), f32),
            vmem((2, GROUP * BLK, BLK), f32),
            vmem((GROUP * BLK, HD), f32),
            vmem((2, PAIRS, GROUP * BLK, 2 * BLK), bf16),
            vmem((2, GROUP * BLK, BLK), bf16),
            dma((5,)),
            dma((2, NCTX)),
            dma((2, NCTX)),
            dma((8,)),
            dma((len(PLAN),)),
            dma((len(PLAN),)),
            dma((len(SIB),)),
            dma((len(SIB),)),
            dma((16,)),
            dma((16,)),
        ],
        compiler_params=pltpu.CompilerParams(
            collective_id=0, has_side_effects=True, vmem_limit_bytes=58 * 2**20
        ),
        cost_estimate=pl.CostEstimate(
            flops=8_000_000_000, bytes_accessed=30_000_000, transcendentals=7_000_000
        ),
        name="sparse_attention_projection",
    )(
        meta,
        queries,
        cache_keys.reshape(CBLK, BLK, HD),
        cache_values.reshape(CBLK, BLK, HD),
        span_keys,
        span_values,
        out_weight,
    )


def solution(mesh):
    placed = (
        P("ctx", "head"),
        P("ctx", "head"),
        P("ctx", "head"),
        P("ctx", "head"),
        P("ctx", "head"),
        P(),
        P(),
        P("head", "ctx"),
    )
    return jax.shard_map(
        per_device, mesh=mesh, in_specs=placed, out_specs=P("ctx", "head"), check_vma=False
    )
```
